32 devices in a mesh: req: 8 (over z, y), tp: 4 (over x, core).
Axes of the slice: x: 2, y: 2, z: 4, core: 2. Of those that a mesh axis runs over, the one named last changes fastest.
Arguments:
- tokens: bfloat16 [4096, 2048], P('req', 'tp')
- lengths: int32 [8, 4], P('req'), may hold values from 1 to 144, 512 in all within a row
- request_adapter_index: int32 [8, 4], P('req'), may hold values from 0 to 15, as said below
- attention_norm_gain: float32 [2048], replicated, may hold values from 0.5 to 1.5
- query_norm_gain: float32 [128], replicated, may hold values from 0.5 to 1.5
- key_norm_gain: float32 [128], replicated, may hold values from 0.5 to 1.5
- feedforward_norm_gain: float32 [2048], replicated, may hold values from 0.5 to 1.5
- query_weight: bfloat16 [2048, 2048], P(None, 'tp'), may hold values from -0.125 to 0.125
- key_weight: bfloat16 [2048, 1024], P(None, 'tp'), may hold values from -0.125 to 0.125
- value_weight: bfloat16 [2048, 1024], P(None, 'tp'), may hold values from -0.125 to 0.125
- output_weight: bfloat16 [2048, 2048], P('tp'), may hold values from -0.125 to 0.125
- gate_weight: bfloat16 [2048, 3072], P(None, 'tp'), may hold values from -0.125 to 0.125
- up_weight: bfloat16 [2048, 3072], P(None, 'tp'), may hold values from -0.125 to 0.125
- down_weight: bfloat16 [3072, 2048], P('tp'), may hold values from -0.109375 to 0.109375
- query_key_value_adapter_input: bfloat16 [16, 48, 2048], P('req', None, 'tp'), may hold values from -0.125 to 0.125
- output_adapter_input: bfloat16 [16, 16, 2048], P('req', None, 'tp'), may hold values from -0.125 to 0.125
- gate_up_adapter_input: bfloat16 [16, 32, 2048], P('req', None, 'tp'), may hold values from -0.125 to 0.125
- down_adapter_input: bfloat16 [16, 16, 3072], P('req', None, 'tp'), may hold values from -0.109375 to 0.109375
- query_adapter_output: bfloat16 [16, 16, 2048], P('req', None, 'tp'), may hold values from -1.5 to 1.5
- key_adapter_output: bfloat16 [16, 16, 1024], P('req', None, 'tp'), may hold values from -1.5 to 1.5
- value_adapter_output: bfloat16 [16, 16, 1024], P('req', None, 'tp'), may hold values from -1.5 to 1.5
- projection_adapter_output: bfloat16 [16, 16, 2048], P('req', None, 'tp'), may hold values from -1.5 to 1.5
- gate_adapter_output: bfloat16 [16, 16, 3072], P('req', None, 'tp'), may hold values from -1.5 to 1.5
- up_adapter_output: bfloat16 [16, 16, 3072], P('req', None, 'tp'), may hold values from -1.5 to 1.5
- down_adapter_output: bfloat16 [16, 16, 2048], P('req', None, 'tp'), may hold values from -1.5 to 1.5
Outputs:
- layer_out: bfloat16 [4096, 2048], P('req', 'tp')
The draws below stay inside these ranges and needn't reach their ends.
Inputs may be any that keep to these rules, and one draw needn't show every extreme that they name: `request_adapter_index`: the 4 requests of one group use adapters of 4 different owners; adapter a belongs to owner a // 2, the index of req that holds it. The lengths of one group's requests sum to 512; the longest is 144.
All inputs are finite; a program needn't handle non-finite values.
Results may differ from the reference program's by a relative error of at most 0.014.
Values may be sent and summed in bfloat16 or wider, within the bound.
No kernel may reach another device: no remote copies, remote signals or barrier semaphores. Data moves between devices by JAX's collectives and lax.ppermute only.
A program may use at most 128 MiB of HBM per device.

```python
import math
import jax
import jax.numpy as jnp
import numpy as np
from jax import lax

MODEL_WIDTH = 2048
QUERY_HEADS = 16
KEY_VALUE_HEADS = 8
HEAD_WIDTH = 128
FEEDFWD_HALF = 3072
ADAPTER_RANK = 16
ADPT_DEV = 2
TOK_DEV = 512
REQ_DEV = 4
MOST_LEN = 144
GROUPS = 8
ADAPTER_TOTAL = 16
TOKENS = 4096


def draw_tokens(key, part):
    first_key, second_key, third_key = jax.random.split(jax.random.fold_in(key, 11), 3)
    column_scale = jnp.exp(jax.random.uniform(second_key, (MODEL_WIDTH,), jnp.float32, math.log(0.3), math.log(3.0)))
    row_scale = jnp.exp(jax.random.uniform(third_key, (TOKENS, 1), jnp.float32, math.log(0.5), math.log(2.0)))
    base_values = jax.random.normal(first_key, (TOKENS, MODEL_WIDTH), jnp.float32)
    return (base_values * column_scale[None, :] * row_scale).astype(jnp.bfloat16)


def draw_request_adapter_index(key, part):
    first_key, second_key = jax.random.split(jax.random.fold_in(key, 23), 2)
    owner_count = ADAPTER_TOTAL // ADPT_DEV
    scores = jax.random.randint(first_key, (GROUPS, owner_count), 0, 1 << 20) * owner_count
    scores = scores + jnp.arange(owner_count, dtype=jnp.int32)[None, :]
    order = jnp.argsort(scores, axis=1)[:, :REQ_DEV].astype(jnp.int32)
    local_pick = jax.random.randint(second_key, (GROUPS, REQ_DEV), 0, ADPT_DEV)
    return (order * ADPT_DEV + local_pick).astype(jnp.int32)


def block_levels(rng, dims, cuts, low, largest):
    factor_of = 1.0
    for dim, parts in cuts:
        heights = jax.random.uniform(jax.random.fold_in(jax.random.fold_in(rng, 6), dim), (parts,), jnp.float32, low / len(cuts), largest / len(cuts))
        factor_of = factor_of * jnp.repeat(jnp.exp(heights), dims[dim] // parts).reshape((-1,) + (1,) * (len(dims) - 1 - dim))
    return factor_of


def length_profile(count, total, most, skew):
    loads = [(1 << 20) // math.isqrt(rank ** skew) + 1 for rank in range(2, count + 1)]
    spare, given = total - most - (count - 1), [1] * (count - 1)
    while spare > 0:
        movable = [i for i in range(count - 1) if given[i] < most]
        pool, budget = sum([loads[i] for i in movable]), spare
        for i in movable:
            more = min(most - given[i], max(1, budget * loads[i] // pool), spare)
            given[i] = given[i] + more
            spare = spare - more
    return np.array([most] + given)


def uneven(rng, number_of, total, reach, lean):
    if number_of == 2:
        one = jax.random.randint(rng, (), max(1, total - reach), min(reach, total - 1) + 1)
        return jnp.stack([one, total - one])
    sizes = jnp.asarray(length_profile(number_of, total, reach, lean), jnp.int32)
    couples = (number_of - 1) // 2
    giver, receiver = sizes[1:1 + 2 * couples:2], sizes[2:2 + 2 * couples:2]
    room = jnp.minimum(giver - 1, reach - receiver)
    shifted = jax.random.randint(jax.random.fold_in(rng, 1), (couples,), 0, 1 << 20) % (room + 1)
    sizes = sizes.at[1:1 + 2 * couples:2].set(giver - shifted).at[2:2 + 2 * couples:2].set(receiver + shifted)
    return sizes[jax.random.permutation(jax.random.fold_in(rng, 2), number_of)]


def scatter_about(rng, shape, width, limit, shards=(), kind=jnp.bfloat16):
    entries = jax.random.normal(rng, shape, jnp.float32) * width
    if len(shards) > 0:
        entries = block_levels(rng, shape, shards, -0.22, 0.18) * entries
    return jnp.clip(entries, min=-limit, max=limit).astype(kind)


def setup_inputs(seed: int = 0) -> dict:
    streams_of = jax.random.split(jax.random.key(seed), 26)
    tokens = draw_tokens(jax.random.fold_in(streams_of[25], 71), 0)
    lengths = jax.vmap(lambda own: uneven(own, REQ_DEV, TOK_DEV, MOST_LEN, 2))(jax.random.split(streams_of[1], GROUPS)).reshape((GROUPS, REQ_DEV)).astype(jnp.int32)
    request_adapter_index = draw_request_adapter_index(jax.random.fold_in(streams_of[25], 71), 0)
    attention_norm_gain = jnp.clip(1.0 + 0.1 * jax.random.normal(streams_of[3], (MODEL_WIDTH,), jnp.float32), 0.5, 1.5)
    query_norm_gain = jnp.clip(1.0 + 0.1 * jax.random.normal(streams_of[4], (HEAD_WIDTH,), jnp.float32), 0.5, 1.5)
    key_norm_gain = jnp.clip(1.0 + 0.1 * jax.random.normal(streams_of[5], (HEAD_WIDTH,), jnp.float32), 0.5, 1.5)
    feedforward_norm_gain = jnp.clip(1.0 + 0.1 * jax.random.normal(streams_of[6], (MODEL_WIDTH,), jnp.float32), 0.5, 1.5)
    query_weight = scatter_about(streams_of[7], (MODEL_WIDTH, QUERY_HEADS * HEAD_WIDTH), MODEL_WIDTH ** -0.5, 0.125, ((1, 4),))
    key_weight = scatter_about(streams_of[8], (MODEL_WIDTH, KEY_VALUE_HEADS * HEAD_WIDTH), MODEL_WIDTH ** -0.5, 0.125, ((1, 4),))
    value_weight = scatter_about(streams_of[9], (MODEL_WIDTH, KEY_VALUE_HEADS * HEAD_WIDTH), MODEL_WIDTH ** -0.5, 0.125, ((1, 4),))
    output_weight = scatter_about(streams_of[10], (QUERY_HEADS * HEAD_WIDTH, MODEL_WIDTH), (QUERY_HEADS * HEAD_WIDTH) ** -0.5, 0.125, ((0, 4),))
    gate_weight = scatter_about(streams_of[11], (MODEL_WIDTH, FEEDFWD_HALF), MODEL_WIDTH ** -0.5, 0.125, ((1, 4),))
    up_weight = scatter_about(streams_of[12], (MODEL_WIDTH, FEEDFWD_HALF), MODEL_WIDTH ** -0.5, 0.125, ((1, 4),))
    down_weight = scatter_about(streams_of[13], (FEEDFWD_HALF, MODEL_WIDTH), FEEDFWD_HALF ** -0.5, 0.109375, ((0, 4),))
    query_key_value_adapter_input = scatter_about(streams_of[14], (ADAPTER_TOTAL, 3 * ADAPTER_RANK, MODEL_WIDTH), MODEL_WIDTH ** -0.5, 0.125, ((0, 8), (2, 4)))
    output_adapter_input = scatter_about(streams_of[15], (ADAPTER_TOTAL, ADAPTER_RANK, QUERY_HEADS * HEAD_WIDTH), (QUERY_HEADS * HEAD_WIDTH) ** -0.5, 0.125, ((0, 8), (2, 4)))
    gate_up_adapter_input = scatter_about(streams_of[16], (ADAPTER_TOTAL, 2 * ADAPTER_RANK, MODEL_WIDTH), MODEL_WIDTH ** -0.5, 0.125, ((0, 8), (2, 4)))
    down_adapter_input = scatter_about(streams_of[17], (ADAPTER_TOTAL, ADAPTER_RANK, FEEDFWD_HALF), FEEDFWD_HALF ** -0.5, 0.109375, ((0, 8), (2, 4)))
    query_adapter_output = scatter_about(streams_of[18], (ADAPTER_TOTAL, ADAPTER_RANK, QUERY_HEADS * HEAD_WIDTH), ADAPTER_RANK ** -0.5, 1.5, ((0, 8), (2, 4)))
    key_adapter_output = scatter_about(streams_of[19], (ADAPTER_TOTAL, ADAPTER_RANK, KEY_VALUE_HEADS * HEAD_WIDTH), ADAPTER_RANK ** -0.5, 1.5, ((0, 8), (2, 4)))
    value_adapter_output = scatter_about(streams_of[20], (ADAPTER_TOTAL, ADAPTER_RANK, KEY_VALUE_HEADS * HEAD_WIDTH), ADAPTER_RANK ** -0.5, 1.5, ((0, 8), (2, 4)))
    projection_adapter_output = scatter_about(streams_of[21], (ADAPTER_TOTAL, ADAPTER_RANK, MODEL_WIDTH), ADAPTER_RANK ** -0.5, 1.5, ((0, 8), (2, 4)))
    gate_adapter_output = scatter_about(streams_of[22], (ADAPTER_TOTAL, ADAPTER_RANK, FEEDFWD_HALF), ADAPTER_RANK ** -0.5, 1.5, ((0, 8), (2, 4)))
    up_adapter_output = scatter_about(streams_of[23], (ADAPTER_TOTAL, ADAPTER_RANK, FEEDFWD_HALF), ADAPTER_RANK ** -0.5, 1.5, ((0, 8), (2, 4)))
    down_adapter_output = scatter_about(streams_of[24], (ADAPTER_TOTAL, ADAPTER_RANK, MODEL_WIDTH), ADAPTER_RANK ** -0.5, 1.5, ((0, 8), (2, 4)))
    return dict(tokens=tokens, lengths=lengths, request_adapter_index=request_adapter_index, attention_norm_gain=attention_norm_gain, query_norm_gain=query_norm_gain, key_norm_gain=key_norm_gain, feedforward_norm_gain=feedforward_norm_gain, query_weight=query_weight, key_weight=key_weight, value_weight=value_weight, output_weight=output_weight, gate_weight=gate_weight, up_weight=up_weight, down_weight=down_weight, query_key_value_adapter_input=query_key_value_adapter_input, output_adapter_input=output_adapter_input, gate_up_adapter_input=gate_up_adapter_input, down_adapter_input=down_adapter_input, query_adapter_output=query_adapter_output, key_adapter_output=key_adapter_output, value_adapter_output=value_adapter_output, projection_adapter_output=projection_adapter_output, gate_adapter_output=gate_adapter_output, up_adapter_output=up_adapter_output, down_adapter_output=down_adapter_output)


epsilon = 1e-06
rope_base = 1000000.0

def rms_scale(values, gain):
    mean_square = lax.optimization_barrier(jnp.mean(values * values, axis=-1, keepdims=True))
    return values * lax.rsqrt(mean_square + epsilon) * gain

def rotate(values, position):
    head_size = values.shape[-1]
    half_size = head_size // 2
    inverse = rope_base ** (-(jnp.arange(half_size, dtype=jnp.float32) * 2.0) / head_size)
    angle = position[:, None] * inverse[None, :]
    cosine = jnp.cos(angle)[:, None, :]
    sine = jnp.sin(angle)[:, None, :]
    first_half = values[..., :half_size]
    second_half = values[..., half_size:]
    return jnp.concatenate([first_half * cosine - second_half * sine, second_half * cosine + first_half * sine], axis=-1)

def request_layout(request_lens, row_count):
    ends = jnp.cumsum(request_lens).astype(jnp.int32)
    starts = (ends - request_lens).astype(jnp.int32)
    row_index = jnp.arange(row_count, dtype=jnp.int32)
    membership_mask = (row_index[:, None] >= starts[None, :]) & (row_index[:, None] < ends[None, :])
    member_int = membership_mask.astype(jnp.int32)
    request = lax.optimization_barrier(jnp.sum(member_int * jnp.arange(request_lens.shape[0], dtype=jnp.int32)[None, :], axis=1))
    position = row_index - lax.optimization_barrier(jnp.sum(member_int * starts[None, :], axis=1))
    return (membership_mask, request, position)

def adapter_update(inputs, membership_mask, a_rows, b_list):
    low_rank = jnp.einsum('tw,jrw->tjr', inputs.astype(jnp.float32), a_rows.astype(jnp.float32))
    low_rank = (low_rank * membership_mask.astype(jnp.float32)[:, :, None]).astype(jnp.bfloat16)
    deltas = []
    offset = 0
    for b_rows in b_list:
        rank_width = b_rows.shape[1]
        piece = low_rank[:, :, offset:offset + rank_width].astype(jnp.float32)
        deltas.append(jnp.einsum('tjr,jro->to', piece, b_rows.astype(jnp.float32)).astype(jnp.bfloat16))
        offset += rank_width
    return deltas

def attend(query, keys, values, request):
    row_count, query_heads, head_size = query.shape
    kv_heads = keys.shape[1]
    grouped = query.reshape(row_count, kv_heads, query_heads // kv_heads, head_size)
    scores = jnp.einsum('tkgd,skd->kgts', grouped.astype(jnp.float32), keys.astype(jnp.float32)) / math.sqrt(head_size)
    row_index = jnp.arange(row_count, dtype=jnp.int32)
    allowed = (request[:, None] == request[None, :]) & (row_index[None, :] <= row_index[:, None])
    raw = jnp.where(allowed[None, None], jnp.exp(scores), 0.0)
    probs = (raw / lax.optimization_barrier(jnp.sum(raw, axis=-1, keepdims=True))).astype(jnp.bfloat16)
    mixed = jnp.einsum('kgts,skd->tkgd', probs.astype(jnp.float32), values.astype(jnp.float32))
    return mixed.reshape(row_count, query_heads * head_size).astype(jnp.bfloat16)

def reference(tokens, lengths, request_adapter_index, attention_norm_gain, query_norm_gain, key_norm_gain, feedforward_norm_gain, query_weight, key_weight, value_weight, output_weight, gate_weight, up_weight, down_weight, query_key_value_adapter_input, output_adapter_input, gate_up_adapter_input, down_adapter_input, query_adapter_output, key_adapter_output, value_adapter_output, projection_adapter_output, gate_adapter_output, up_adapter_output, down_adapter_output):
    blocks = tokens.reshape(GROUPS, TOK_DEV, MODEL_WIDTH)

    def one_block(items):
        block, request_lens, request_index_list = items
        membership_mask, request, position = request_layout(request_lens, TOK_DEV)
        pos_float = position.astype(jnp.float32)
        attention_normalized = rms_scale(block.astype(jnp.float32), attention_norm_gain).astype(jnp.bfloat16)
        query_update, key_update, value_update = adapter_update(attention_normalized, membership_mask, query_key_value_adapter_input[request_index_list], [query_adapter_output[request_index_list], key_adapter_output[request_index_list], value_adapter_output[request_index_list]])
        query = jnp.dot(attention_normalized, query_weight, preferred_element_type=jnp.float32) + query_update.astype(jnp.float32)
        query = rotate(rms_scale(query.reshape(TOK_DEV, QUERY_HEADS, HEAD_WIDTH), query_norm_gain), pos_float).astype(jnp.bfloat16)
        keys = jnp.dot(attention_normalized, key_weight, preferred_element_type=jnp.float32) + key_update.astype(jnp.float32)
        keys = rotate(rms_scale(keys.reshape(TOK_DEV, KEY_VALUE_HEADS, HEAD_WIDTH), key_norm_gain), pos_float).astype(jnp.bfloat16)
        values = (jnp.dot(attention_normalized, value_weight, preferred_element_type=jnp.float32) + value_update.astype(jnp.float32)).astype(jnp.bfloat16)
        attention_result = attend(query, keys, values.reshape(TOK_DEV, KEY_VALUE_HEADS, HEAD_WIDTH), request)
        output_update = adapter_update(attention_result, membership_mask, output_adapter_input[request_index_list], [projection_adapter_output[request_index_list]])[0]
        resid = jnp.dot(attention_result, output_weight, preferred_element_type=jnp.float32) + output_update.astype(jnp.float32) + block.astype(jnp.float32)
        resid = resid.astype(jnp.bfloat16)
        feedforward_normalized = rms_scale(resid.astype(jnp.float32), feedforward_norm_gain).astype(jnp.bfloat16)
        gate_update, up_update = adapter_update(feedforward_normalized, membership_mask, gate_up_adapter_input[request_index_list], [gate_adapter_output[request_index_list], up_adapter_output[request_index_list]])
        gate = jnp.dot(feedforward_normalized, gate_weight, preferred_element_type=jnp.float32) + gate_update.astype(jnp.float32)
        upward = jnp.dot(feedforward_normalized, up_weight, preferred_element_type=jnp.float32) + up_update.astype(jnp.float32)
        hidden_state = (jax.nn.silu(gate) * upward).astype(jnp.bfloat16)
        down_update = adapter_update(hidden_state, membership_mask, down_adapter_input[request_index_list], [down_adapter_output[request_index_list]])[0]
        result = jnp.dot(hidden_state, down_weight, preferred_element_type=jnp.float32) + down_update.astype(jnp.float32) + resid.astype(jnp.float32)
        return result.astype(jnp.bfloat16)
    outputs = lax.map(one_block, (blocks, lengths, request_adapter_index))
    return outputs.reshape(TOKENS, MODEL_WIDTH)
```

```python
import functools
import math

import jax
import jax.numpy as jnp
from jax import lax
from jax.experimental import pallas as pl
from jax.experimental.pallas import tpu as pltpu
from jax.sharding import PartitionSpec as P

HEAD_WIDTH = 128
CHUNKS = 2

epsilon = 1e-06
rope_base = 1000000.0

bf16 = jnp.bfloat16
f32 = jnp.float32
VMEM = pl.BlockSpec(memory_space=pltpu.VMEM)
SMEM = pl.BlockSpec(memory_space=pltpu.SMEM)


def call(body, in_specs, outs, flops=0, moved=0, scratch=(), limit=40):
    single = not isinstance(outs, (list, tuple))
    listed = [outs] if single else list(outs)
    return pl.pallas_call(
        body,
        out_shape=outs if single else listed,
        in_specs=in_specs,
        out_specs=VMEM if single else [VMEM] * len(listed),
        scratch_shapes=list(scratch),
        compiler_params=pltpu.CompilerParams(vmem_limit_bytes=limit * 1024 * 1024),
        cost_estimate=pl.CostEstimate(flops=flops, bytes_accessed=moved, transcendentals=0),
    )


def shaped(shape, dtype):
    return jax.ShapeDtypeStruct(shape, dtype)


def dot(a, b):
    return lax.dot_general(a, b, (((1,), (0,)), ((), ())), preferred_element_type=f32)


def dot_nt(a, b):
    return lax.dot_general(a, b, (((1,), (1,)), ((), ())), preferred_element_type=f32)


def dot_tn(a, b):
    return lax.dot_general(a, b, (((0,), (0,)), ((), ())), preferred_element_type=f32)


def part_of(index_ref, rel, width):
    return pl.ds(pl.multiple_of((index_ref[0] ^ rel) * width, width), width)


def bounds(lens_ref, count):
    starts, total = [], jnp.int32(0)
    for j in range(count):
        starts.append(total)
        total = total + lens_ref[0, j]
    return starts, starts[1:] + [total]


def lane_masks(lens_ref, count, first, width):
    starts, ends = bounds(lens_ref, count)
    rows = lax.broadcasted_iota(jnp.int32, (1, width), 1) + first
    return [((rows >= s) & (rows < e)).astype(f32) for s, e in zip(starts, ends)]


def pack_first(me_ref, idx_ref, qkv_a, out_a, proj_b, q_b, k_b, v_b, send):
    groups, wanted = idx_ref.shape
    held, low, _ = qkv_a.shape
    rank = out_a.shape[1]
    k_width = k_b.shape[2]

    @pl.loop(0, groups)
    def _(g):
        pick = jnp.int32(0)
        for j in range(wanted):
            a = idx_ref[g, j]
            pick = pick + jnp.where(a // held == me_ref[0], a % held, 0)
        send[g, 0:low, :] = qkv_a[pick]
        send[g, low : low + rank, :] = out_a[pick]
        send[g, low + rank : low + 2 * rank, :] = proj_b[pick]
        send[g, low + 2 * rank : low + 3 * rank, :] = q_b[pick]
        send[g, low + 3 * rank : low + 4 * rank, 0:k_width] = k_b[pick]
        send[g, low + 3 * rank : low + 4 * rank, k_width:] = v_b[pick]


def pack_second(me_ref, idx_ref, gu_a, down_b, down_a, gate_b, up_b, send):
    groups, wanted = idx_ref.shape
    held = gu_a.shape[0]
    unit = send.shape[2]

    @pl.loop(0, groups)
    def _(g):
        pick = jnp.int32(0)
        for j in range(wanted):
            a = idx_ref[g, j]
            pick = pick + jnp.where(a // held == me_ref[0], a % held, 0)
        row = 0
        for table in (gu_a, down_b, down_a, gate_b, up_b):
            height, width = table.shape[1:]
            for k in range(width // unit):
                send[g, row : row + height, :] = table[pick, :, k * unit : (k + 1) * unit]
                row += height


def rel_owner(want_ref, held, j):
    return want_ref[0, j] // held


def project_qkv(index_ref, own, core, across, diagonal, gain, q_w, k_w, v_w, normed_own, *qkv_outs):
    rows, width = own.shape
    q_width, k_width = q_w.shape[1], k_w.shape[1]
    step = rows // len(qkv_outs)
    for c, out in enumerate(qkv_outs):
        here = slice(c * step, (c + 1) * step)
        blocks = [ref[here, :].astype(f32) for ref in (own, core, across, diagonal)]
        square = sum(jnp.sum(b * b, axis=1, keepdims=True) for b in blocks)
        scale = lax.rsqrt(square / (4 * width) + epsilon)
        for rel, block in enumerate(blocks):
            part = part_of(index_ref, rel, width)
            normed = (block * scale * gain[:, part]).astype(bf16)
            if rel == 0:
                normed_own[here, :] = normed
            for w, low, high in (
                (q_w, 0, q_width),
                (k_w, q_width, q_width + k_width),
                (v_w, q_width + k_width, q_width + 2 * k_width),
            ):
                term = dot(normed, w[part, :])
                if rel == 0:
                    out[:, low:high] = term
                else:
                    out[:, low:high] += term


def low_first(held, low, rank, want_ref, lens_ref, received, normed_own, out, stack):
    wanted = want_ref.shape[1]
    for j in range(wanted):
        owner = rel_owner(want_ref, held, j)
        stack[j * low : (j + 1) * low, :] = received[owner, 0:low, :]
        out[low + j * rank : low + (j + 1) * rank, :] = received[owner, low + rank : low + 2 * rank, :]
    products = dot_nt(stack[...], normed_own[...])
    masks = lane_masks(lens_ref, wanted, 0, normed_own.shape[0])
    out[0:low, :] = sum(
        products[j * low : (j + 1) * low, :] * masks[j] for j in range(wanted)
    ).astype(bf16)


def attend(
    chunk, held, low, rank, heads, kv_heads,
    index_ref, want_ref, lens_ref, qkv, shared0, shared1, shared2, shared3, received, cosine, sine,
    q_gain, k_gain, out_w, old_k, old_v, keep, send, new_k, new_v, stack_q, stack_k, stack_v, stack_o,
):
    rows = qkv.shape[0]
    width = out_w.shape[0]
    first = chunk * rows
    here = slice(first, first + rows)
    wanted = want_ref.shape[1]
    shared = (shared0, shared1, shared2, shared3)
    q_width, k_width = heads * HEAD_WIDTH, kv_heads * HEAD_WIDTH
    for j in range(wanted):
        owner = rel_owner(want_ref, held, j)
        at = slice(j * rank, (j + 1) * rank)
        stack_o[at, :] = received[owner, low : low + rank, :]
        stack_q[at, :] = received[owner, low + 2 * rank : low + 3 * rank, :]
        stack_k[at, :] = received[owner, low + 3 * rank : low + 4 * rank, 0:k_width]
        stack_v[at, :] = received[owner, low + 3 * rank : low + 4 * rank, k_width:]
    masks = lane_masks(lens_ref, wanted, first, rows)
    total = sum(ref[0:low, here].astype(f32) for ref in shared).astype(bf16).astype(f32)

    def delta(number, stack):
        piece = total[number * rank : (number + 1) * rank, :]
        spread = jnp.concatenate([piece * m for m in masks], axis=0).astype(bf16)
        return dot_tn(spread, stack[...]).astype(bf16).astype(f32)

    query = qkv[:, 0:q_width] + delta(0, stack_q)
    key = qkv[:, q_width : q_width + k_width] + delta(1, stack_k)
    new_v[...] = (qkv[:, q_width + k_width :] + delta(2, stack_v)).astype(bf16)
    cos, sin = cosine[here, :], sine[here, :]

    def turn(values, gain):
        square = jnp.mean(values * values, axis=1, keepdims=True)
        values = values * lax.rsqrt(square + epsilon) * gain[...]
        return (values * cos + pltpu.roll(values, HEAD_WIDTH // 2, 1) * sin).astype(bf16)

    def head(h):
        return slice(h * HEAD_WIDTH, (h + 1) * HEAD_WIDTH)

    for h in range(kv_heads):
        new_k[:, head(h)] = turn(key[:, head(h)], k_gain)
    seen = first + rows
    starts, _ = bounds(lens_ref, wanted)
    down = lax.broadcasted_iota(jnp.int32, (rows, 1), 0) + first
    start_of = jnp.zeros((rows, 1), jnp.int32)
    for s in starts:
        start_of = jnp.where(down >= s, s, start_of)
    along = lax.broadcasted_iota(jnp.int32, (rows, seen), 1)
    allowed = (along <= down) & (along >= start_of)
    group = heads // kv_heads
    mixed = []
    for kv in range(kv_heads):
        keys, values = new_k[:, head(kv)], new_v[:, head(kv)]
        if chunk > 0:
            keys = jnp.concatenate([old_k[:, head(kv)], keys], axis=0)
            values = jnp.concatenate([old_v[:, head(kv)], values], axis=0)
        for h in range(kv * group, (kv + 1) * group):
            scores = dot_nt(turn(query[:, head(h)], q_gain), keys) * (1.0 / math.sqrt(HEAD_WIDTH))
            raw = jnp.where(allowed, jnp.exp(scores), 0.0)
            probs = (raw / jnp.sum(raw, axis=1, keepdims=True)).astype(bf16)
            mixed.append(dot(probs, values).astype(bf16))
    attended = jnp.concatenate(mixed, axis=1)
    lows = dot_nt(stack_o[...], attended)
    lows = jnp.concatenate(
        [lows[j * rank : (j + 1) * rank, :] * masks[j] for j in range(wanted)], axis=0
    ).astype(bf16)
    for rel in range(4):
        part = part_of(index_ref, rel, width)
        table = shared[rel][low : low + wanted * rank, :]
        term = dot(attended, out_w[:, part]) + dot_tn(lows, table)
        target, at = ((keep, 0), (send, 0), (keep, 1), (send, 1))[rel]
        target[:, at * width : (at + 1) * width] = term.astype(target.dtype)


def add_pair(kept, arrived, out):
    out[...] = (kept[...] + arrived[...].astype(f32)).astype(bf16)


def residual(chunk, chip, arrived, own, across, out):
    rows = chip.shape[0]
    width = own.shape[1]
    here = slice(chunk * rows, (chunk + 1) * rows)
    left, right = slice(0, width), slice(width, 2 * width)
    for mine, theirs, tokens in ((left, right, own), (right, left, across)):
        total = chip[:, mine].astype(f32) + arrived[:, theirs].astype(f32)
        out[:, mine] = (total + tokens[here, :].astype(f32)).astype(bf16)


def choose_second(held, low, rank, want_ref, received, out):
    wanted = want_ref.shape[1]
    unit = received.shape[2]
    for j in range(wanted):
        owner = rel_owner(want_ref, held, j)
        row = 0
        for base, height in ((0, low), (wanted * low, rank)):
            at = slice(base + j * height, base + (j + 1) * height)
            for k in range(out.shape[1] // unit):
                out[at, k * unit : (k + 1) * unit] = received[owner, row : row + height, :]
                row += height


def feed_forward(
    chunk, held, low, rank,
    index_ref, want_ref, lens_ref, mine, theirs, table0, table1, table2, table3, received, gain,
    gate_w, up_w, down_w, keep, send, stack_a, stack_g, stack_u,
):
    rows = mine.shape[0]
    width = mine.shape[1] // 2
    hidden_width = gate_w.shape[1]
    first = chunk * rows
    wanted = want_ref.shape[1]
    unit = received.shape[2]
    tables = (table0, table1, table2, table3)
    for j in range(wanted):
        owner = rel_owner(want_ref, held, j)
        at = slice(j * rank, (j + 1) * rank)
        row = (low + rank) * (width // unit)
        for stack in (stack_a, stack_g, stack_u):
            for k in range(hidden_width // unit):
                stack[at, k * unit : (k + 1) * unit] = received[owner, row : row + rank, :]
                row += rank
    masks = lane_masks(lens_ref, wanted, first, rows)
    blocks = [
        ref[:, at * width : (at + 1) * width].astype(f32)
        for ref, at in ((mine, 0), (theirs, 0), (mine, 1), (theirs, 1))
    ]
    square = sum(jnp.sum(b * b, axis=1, keepdims=True) for b in blocks)
    scale = lax.rsqrt(square / (4 * width) + epsilon)
    gate = upward = products = None
    for rel, block in enumerate(blocks):
        part = part_of(index_ref, rel, width)
        normed = (block * scale * gain[:, part]).astype(bf16)
        terms = (
            dot(normed, gate_w[part, :]),
            dot(normed, up_w[part, :]),
            dot_nt(tables[rel][0 : wanted * low, :], normed),
        )
        if rel == 0:
            gate, upward, products = terms
        else:
            gate, upward, products = gate + terms[0], upward + terms[1], products + terms[2]
    total = sum(products[j * low : (j + 1) * low, :] * masks[j] for j in range(wanted))
    total = total.astype(bf16).astype(f32)

    def delta(number, stack):
        piece = total[number * rank : (number + 1) * rank, :]
        spread = jnp.concatenate([piece * m for m in masks], axis=0).astype(bf16)
        return dot_tn(spread, stack[...]).astype(bf16).astype(f32)

    gate = gate + delta(0, stack_g)
    upward = upward + delta(1, stack_u)
    hidden = (gate / (1.0 + jnp.exp(-gate)) * upward).astype(bf16)
    lows = dot_nt(stack_a[...], hidden)
    lows = jnp.concatenate(
        [lows[j * rank : (j + 1) * rank, :] * masks[j] for j in range(wanted)], axis=0
    ).astype(bf16)
    for rel in range(4):
        part = part_of(index_ref, rel, width)
        table = tables[rel][wanted * low : wanted * (low + rank), :]
        term = dot(hidden, down_w[:, part]) + dot_tn(lows, table)
        target, at = ((keep, 0), (send, 0), (keep, 1), (send, 1))[rel]
        target[:, at * width : (at + 1) * width] = term.astype(target.dtype)


def split_pair(kept, arrived, stay, away):
    width = stay.shape[1]
    stay[...] = kept[:, 0:width] + arrived[:, 0:width].astype(f32)
    away[...] = (kept[:, width:] + arrived[:, width:].astype(f32)).astype(bf16)


def finish(count, *refs):
    out = refs[-1]
    for c in range(count):
        stay, arrived, resid = refs[3 * c : 3 * c + 3]
        rows, width = stay.shape
        total = stay[...] + arrived[...].astype(f32) + resid[:, 0:width].astype(f32)
        out[c * rows : (c + 1) * rows, :] = total.astype(bf16)


def rotation_tables(lens, row_count):
    half = HEAD_WIDTH // 2
    inverse = rope_base ** (-(jnp.arange(half, dtype=f32) * 2.0) / HEAD_WIDTH)
    row = jnp.arange(row_count, dtype=jnp.int32)
    start_of = jnp.zeros_like(row)
    start = jnp.int32(0)
    for j in range(lens.shape[0]):
        start_of = jnp.where(row >= start, start, start_of)
        start = start + lens[j]
    angle = (row - start_of).astype(f32)[:, None] * jnp.concatenate([inverse, inverse])[None, :]
    sign = jnp.concatenate([-jnp.ones(half, f32), jnp.ones(half, f32)])
    return jnp.cos(angle), jnp.sin(angle) * sign[None, :]


def swap_core(values):
    return lax.ppermute(values, "tp", [(k, k ^ 1) for k in range(4)])


def swap_across(values):
    return lax.ppermute(values, "tp", [(k, k ^ 2) for k in range(4)])


def swap_diagonal(values):
    return lax.ppermute(values, "tp", [(k, k ^ 3) for k in range(4)])


def to_groups(values):
    return lax.all_to_all(values, "req", split_axis=0, concat_axis=0, tiled=True)


def per_device(
    tokens,
    lengths,
    request_adapter_index,
    attention_norm_gain,
    query_norm_gain,
    key_norm_gain,
    feedforward_norm_gain,
    query_weight,
    key_weight,
    value_weight,
    output_weight,
    gate_weight,
    up_weight,
    down_weight,
    query_key_value_adapter_input,
    output_adapter_input,
    gate_up_adapter_input,
    down_adapter_input,
    query_adapter_output,
    key_adapter_output,
    value_adapter_output,
    projection_adapter_output,
    gate_adapter_output,
    up_adapter_output,
    down_adapter_output,
):
    assert lax.axis_size("tp") == 4
    row_count, width = tokens.shape
    groups = lax.axis_size("req")
    wanted = lengths.shape[1]
    held, low_qkv, _ = query_key_value_adapter_input.shape
    rank = output_adapter_input.shape[1]
    low_gu = gate_up_adapter_input.shape[1]
    q_width, k_width = query_weight.shape[1], key_weight.shape[1]
    hidden_width = gate_weight.shape[1]
    heads, kv_heads = q_width // HEAD_WIDTH, k_width // HEAD_WIDTH
    assert row_count == width == q_width == 2 * k_width
    unit = math.gcd(width, hidden_width)
    rows = row_count // CHUNKS
    index = lax.axis_index("tp").astype(jnp.int32).reshape(1)
    me = lax.axis_index("req").astype(jnp.int32).reshape(1)

    asked = to_groups(jnp.broadcast_to(request_adapter_index, (groups, wanted)))
    first_rows = low_qkv + 4 * rank
    send_first = call(
        pack_first, [SMEM, SMEM] + [VMEM] * 6, shaped((groups, first_rows, width), bf16),
        moved=2 * groups * first_rows * width,
    )(
        me, asked, query_key_value_adapter_input, output_adapter_input, projection_adapter_output,
        query_adapter_output, key_adapter_output, value_adapter_output,
    )
    received = to_groups(send_first)

    across = swap_across(tokens)
    core = swap_core(tokens)
    diagonal = swap_core(across)
    gain_one = attention_norm_gain.reshape(1, -1)
    gain_two = feedforward_norm_gain.reshape(1, -1)
    q_gain = query_norm_gain.reshape(1, -1)
    k_gain = key_norm_gain.reshape(1, -1)
    qkv_width = q_width + 2 * k_width
    normed_own, *qkv = call(
        project_qkv, [SMEM] + [VMEM] * 8,
        [shaped((row_count, width), bf16)] + [shaped((rows, qkv_width), f32)] * CHUNKS,
        flops=2 * row_count * 4 * width * qkv_width, moved=8 * width * qkv_width,
    )(index, tokens, core, across, diagonal, gain_one, query_weight, key_weight, value_weight)

    asked, normed_own = lax.optimization_barrier((asked, normed_own))
    second_rows = ((low_gu + rank) * width + 3 * rank * hidden_width) // unit
    send_second = call(
        pack_second, [SMEM, SMEM] + [VMEM] * 5, shaped((groups, second_rows, unit), bf16),
        moved=2 * groups * second_rows * unit,
    )(
        me, asked, gate_up_adapter_input, down_adapter_output, down_adapter_input,
        gate_adapter_output, up_adapter_output,
    )
    received_second = to_groups(send_second)

    cosine, sine = rotation_tables(lengths[0], row_count)
    shared_own = call(
        functools.partial(low_first, held, low_qkv, rank), [SMEM, SMEM, VMEM, VMEM],
        shaped((low_qkv + wanted * rank, width), bf16),
        flops=2 * wanted * low_qkv * width * row_count, moved=2 * row_count * width,
        scratch=[pltpu.VMEM((wanted * low_qkv, width), bf16)],
    )(request_adapter_index, lengths, received, normed_own)
    shared = (shared_own, swap_core(shared_own), swap_across(shared_own), swap_diagonal(shared_own))

    table = call(
        functools.partial(choose_second, held, low_gu, rank), [SMEM, VMEM],
        shaped((wanted * (low_gu + rank), width), bf16),
        moved=4 * wanted * (low_gu + rank) * width,
    )(request_adapter_index, received_second)
    table_across = swap_across(table)
    tables = (table, swap_core(table), table_across, swap_core(table_across))

    wide = shaped((rows, 2 * width), bf16)
    kept = shaped((rows, 2 * width), f32)
    old_k = old_v = None
    chips = []
    for c in range(CHUNKS):
        if c == 0:
            past = [jnp.zeros((16, k_width), bf16)] * 2
        else:
            past = [old_k, old_v]
        keep, send, new_k, new_v = call(
            functools.partial(attend, c, held, low_qkv, rank, heads, kv_heads),
            [SMEM] * 3 + [VMEM] * 13,
            [kept, wide, shaped((rows, k_width), bf16), shaped((rows, k_width), bf16)],
            flops=2 * rows * width * 4 * width + 4 * heads * rows * row_count * HEAD_WIDTH,
            moved=8 * width * width,
            scratch=[
                pltpu.VMEM((wanted * rank, q_width), bf16),
                pltpu.VMEM((wanted * rank, k_width), bf16),
                pltpu.VMEM((wanted * rank, k_width), bf16),
                pltpu.VMEM((wanted * rank, width), bf16),
            ],
        )(
            index, request_adapter_index, lengths, qkv[c], *shared, received, cosine, sine,
            q_gain, k_gain, output_weight, *past,
        )
        if c == 0:
            old_k, old_v = new_k, new_v
        else:
            old_k = jnp.concatenate([old_k, new_k], axis=0)
            old_v = jnp.concatenate([old_v, new_v], axis=0)
        chips.append((keep, swap_core(send)))

    residuals = []
    for c in range(CHUNKS):
        chip = call(add_pair, [VMEM] * 2, wide, moved=8 * rows * width)(*chips[c])
        resid = call(functools.partial(residual, c), [VMEM] * 4, wide, moved=8 * rows * width)(
            chip, swap_across(chip), tokens, across
        )
        residuals.append((resid, swap_core(resid)))

    ends = []
    for c in range(CHUNKS):
        keep, send = call(
            functools.partial(feed_forward, c, held, low_gu, rank),
            [SMEM] * 3 + [VMEM] * 11,
            [kept, wide],
            flops=2 * rows * 4 * width * hidden_width * 3,
            moved=2 * 4 * width * hidden_width * 3,
            scratch=[pltpu.VMEM((wanted * rank, hidden_width), bf16)] * 3,
        )(
            index, request_adapter_index, lengths, *residuals[c], *tables, received_second,
            gain_two, gate_weight, up_weight, down_weight,
        )
        stay, away = call(
            split_pair, [VMEM] * 2,
            [shaped((rows, width), f32), shaped((rows, width), bf16)], moved=8 * rows * width,
        )(keep, swap_core(send))
        ends += [stay, swap_across(away), residuals[c][0]]
    return call(
        functools.partial(finish, CHUNKS), [VMEM] * (3 * CHUNKS), shaped((row_count, width), bf16),
        moved=8 * row_count * width,
    )(*ends)


def solution(mesh):
    placed = (
        P("req", "tp"),
        P("req", None),
        P("req", None),
        P(),
        P(),
        P(),
        P(),
        P(None, "tp"),
        P(None, "tp"),
        P(None, "tp"),
        P("tp", None),
        P(None, "tp"),
        P(None, "tp"),
        P("tp", None),
        P("req", None, "tp"),
        P("req", None, "tp"),
        P("req", None, "tp"),
        P("req", None, "tp"),
        P("req", None, "tp"),
        P("req", None, "tp"),
        P("req", None, "tp"),
        P("req", None, "tp"),
        P("req", None, "tp"),
        P("req", None, "tp"),
        P("req", None, "tp"),
    )
    return jax.shard_map(
        per_device, mesh=mesh, in_specs=placed, out_specs=P("req", "tp"), check_vma=False
    )
```

```python
import functools
import math

import jax
import jax.numpy as jnp
from jax import lax
from jax.experimental import pallas as pl
from jax.experimental.pallas import tpu as pltpu
from jax.sharding import PartitionSpec as P

HEAD_WIDTH = 128
CHUNKS = 2

epsilon = 1e-06
rope_base = 1000000.0

bf16 = jnp.bfloat16
f32 = jnp.float32
VMEM = pl.BlockSpec(memory_space=pltpu.VMEM)
ANY = pl.BlockSpec(memory_space=pl.ANY)
HBM = pl.BlockSpec(memory_space=pltpu.HBM)
SMEM = pl.BlockSpec(memory_space=pltpu.SMEM)


def call(body, in_specs, outs, scratch=(), limit=16, out_specs=None):
    single = not isinstance(outs, (list, tuple))
    if out_specs is None:
        out_specs = VMEM if single else [VMEM] * len(outs)
    return pl.pallas_call(
        body,
        out_shape=outs if single else list(outs),
        in_specs=in_specs,
        out_specs=out_specs,
        scratch_shapes=list(scratch),
        compiler_params=pltpu.CompilerParams(vmem_limit_bytes=limit * 1024 * 1024),
        cost_estimate=pl.CostEstimate(flops=1, bytes_accessed=1, transcendentals=0),
    )


def shaped(shape, dtype):
    return jax.ShapeDtypeStruct(shape, dtype)


def dot(a, b):
    return lax.dot_general(a, b, (((1,), (0,)), ((), ())), preferred_element_type=f32)


def dot_nt(a, b):
    return lax.dot_general(a, b, (((1,), (1,)), ((), ())), preferred_element_type=f32)


def dot_tn(a, b):
    return lax.dot_general(a, b, (((0,), (0,)), ((), ())), preferred_element_type=f32)


def part_of(index_ref, rel, width):
    return pl.ds(pl.multiple_of((index_ref[0] ^ rel) * width, width), width)


def bounds(lens_ref, count):
    starts, total = [], jnp.int32(0)
    for j in range(count):
        starts.append(total)
        total = total + lens_ref[0, j]
    return starts, starts[1:] + [total]


def lane_masks(lens_ref, count, first, width):
    starts, ends = bounds(lens_ref, count)
    rows = lax.broadcasted_iota(jnp.int32, (1, width), 1) + first
    return [((rows >= s) & (rows < e)).astype(f32) for s, e in zip(starts, ends)]


def spread(piece, masks):
    return jnp.concatenate([piece * m for m in masks], axis=0).astype(bf16)


def merged(products, masks, low):
    return sum(products[j * low : (j + 1) * low, :] * m for j, m in enumerate(masks))


def delta(piece, masks, stack):
    return dot_tn(spread(piece, masks), stack).astype(bf16).astype(f32)


def start_all(pairs, sems):
    copies = [pltpu.make_async_copy(a, b, sems.at[k]) for k, (a, b) in enumerate(pairs)]
    for copy in copies:
        copy.start()
    return copies


def gather_tables(plans, *refs):
    *refs, sems = refs
    pairs = []
    for plan, out in zip(plans, refs[-len(plans) :]):
        for table, columns, row, column in plan:
            source = refs[table]
            there = out.at[:, pl.ds(row, source.shape[1]), pl.ds(column, columns[1])]
            pairs.append((source.at[:, :, pl.ds(*columns)], there))
    for copy in start_all(pairs, sems):
        copy.wait()


def load(count, *refs):
    for copy in start_all(list(zip(refs[:count], refs[-1 - count : -1])), refs[-1]):
        copy.wait()


def owner_at(me_ref, rel, flip):
    return me_ref[0] ^ (2 * rel + flip)


def pick_for_neighbour(me_ref, want_ref, *refs):
    *packed, after, send = refs
    held = packed[0].shape[0]
    for rel, ref in enumerate(packed):
        owner = owner_at(me_ref, rel, 0)
        pick = jnp.int32(0)
        for j in range(want_ref.shape[1]):
            a = want_ref[0, j]
            pick = pick + jnp.where(a // held == owner, a % held, 0)
        send[rel] = ref[pick]


def hold(block, after, out):
    out[...] = block[...]


def each_asked(me_ref, want_ref, packed, passed, use):
    held = packed[0].shape[0]
    for rel, ref in enumerate(packed):
        for flip in range(2):
            owner = owner_at(me_ref, rel, flip)
            slot, pick, found = jnp.int32(0), jnp.int32(0), jnp.int32(0)
            for j in range(want_ref.shape[1]):
                a = want_ref[0, j]
                hit = (a // held == owner).astype(jnp.int32)
                slot, pick, found = slot + hit * j, pick + hit * (a % held), found + hit

            @pl.when(found > 0)
            def _():
                use(slot, passed.at[rel] if flip else ref.at[pick])


def normalize(index_ref, refs, gain, normed, keep_own=None):
    blocks = [load() for load in refs]
    width = blocks[0].shape[1]
    square = sum(jnp.sum(b * b, axis=1, keepdims=True) for b in blocks)
    scale = lax.rsqrt(square / (len(blocks) * width) + epsilon)
    for rel, block in enumerate(blocks):
        part = part_of(index_ref, rel, width)
        value = (block * scale * gain[:, part]).astype(bf16)
        normed[:, part] = value
        if rel == 0 and keep_own is not None:
            keep_own(value)


def project_qkv(
    index_ref, own, core, across, diagonal, gain, q_hbm, k_hbm, v_hbm, out_hbm, cosine, sine,
    normed_own, out_w, *rest,
):
    *outs, normed, q_w, k_w, v_w, sems = rest
    copies = start_all([(q_hbm, q_w), (k_hbm, k_w), (v_hbm, v_w), (out_hbm, out_w)], sems)
    rows = own.shape[0] // len(outs)
    q_width, k_width = q_w.shape[1], k_w.shape[1]
    for c in range(len(outs)):
        here = slice(c * rows, (c + 1) * rows)

        def keep_own(value):
            normed_own[here, :] = value

        loads = [lambda ref=ref: ref[here, :].astype(f32) for ref in (own, core, across, diagonal)]
        normalize(index_ref, loads, gain, normed.at[here, :], keep_own)
    for w, copy, low, high in (
        (q_w, copies[0], 0, q_width),
        (k_w, copies[1], q_width, q_width + k_width),
        (v_w, copies[2], q_width + k_width, q_width + 2 * k_width),
    ):
        copy.wait()
        for c, out in enumerate(outs):
            out[:, low:high] = dot(normed[c * rows : (c + 1) * rows, :], w[...])
    copies[3].wait()


def rows_of(slot, height):
    return pl.ds(pl.multiple_of(slot * height, 16), height)


def low_first(rank, me_ref, want_ref, lens_ref, *refs):
    *packed, passed, normed_own, out, chosen, proj, stack = refs
    wanted = want_ref.shape[1]
    low = out.shape[0]

    def use(slot, block):
        stack[rows_of(slot, low), :] = block[0:low, :]
        chosen[slot] = block[low : low + 3 * rank, :]
        proj[rows_of(slot, rank), :] = block[low + 3 * rank :, :]

    each_asked(me_ref, want_ref, packed, passed, use)
    products = dot_nt(stack[...], normed_own[...])
    masks = lane_masks(lens_ref, wanted, 0, normed_own.shape[0])
    out[...] = merged(products, masks, low).astype(bf16)


def attend(
    chunk, heads, kv_heads,
    index_ref, lens_ref, qkv, low0, low1, low2, low3, chosen, cosine, sine,
    q_gain, k_gain, out_w, old_k, old_v, after,
    new_k, new_v, *terms,
):
    rows = qkv.shape[0]
    width = out_w.shape[0]
    first = chunk * rows
    here = slice(first, first + rows)
    wanted, rank = chosen.shape[0], chosen.shape[1] // 3
    q_width, k_width = heads * HEAD_WIDTH, kv_heads * HEAD_WIDTH

    def stack(number, columns=slice(None)):
        block = chosen[:, number * rank : (number + 1) * rank, columns]
        return block.reshape(wanted * rank, block.shape[2])

    masks = lane_masks(lens_ref, wanted, first, rows)
    total = sum(ref[:, here].astype(f32) for ref in (low0, low1, low2, low3))
    total = total.astype(bf16).astype(f32)
    query = qkv[:, 0:q_width] + delta(total[0:rank], masks, stack(0))
    key = qkv[:, q_width : q_width + k_width] + delta(total[rank : 2 * rank], masks, stack(1, slice(0, k_width)))
    value = qkv[:, q_width + k_width :] + delta(total[2 * rank :], masks, stack(1, slice(k_width, 2 * k_width)))
    new_v[...] = value.astype(bf16)
    cos, sin = cosine[here, :], sine[here, :]

    def turn(values, gain):
        square = jnp.mean(values * values, axis=1, keepdims=True)
        values = values * lax.rsqrt(square + epsilon) * gain[...]
        return (values * cos + pltpu.roll(values, HEAD_WIDTH // 2, 1) * sin).astype(bf16)

    def head(h):
        return slice(h * HEAD_WIDTH, (h + 1) * HEAD_WIDTH)

    for h in range(kv_heads):
        new_k[:, head(h)] = turn(key[:, head(h)], k_gain)
    seen = first + rows
    starts, _ = bounds(lens_ref, wanted)
    down = lax.broadcasted_iota(jnp.int32, (rows, 1), 0) + first
    start_of = jnp.zeros((rows, 1), jnp.int32)
    for s in starts:
        start_of = jnp.where(down >= s, s, start_of)
    along = lax.broadcasted_iota(jnp.int32, (rows, seen), 1)
    allowed = (along <= down) & (along >= start_of)
    group = heads // kv_heads
    mixed = []
    for kv in range(kv_heads):
        keys, values = new_k[:, head(kv)], new_v[:, head(kv)]
        if chunk > 0:
            keys = jnp.concatenate([old_k[:, head(kv)], keys], axis=0)
            values = jnp.concatenate([old_v[:, head(kv)], values], axis=0)
        for h in range(kv * group, (kv + 1) * group):
            scores = dot_nt(turn(query[:, head(h)], q_gain), keys) * (1.0 / math.sqrt(HEAD_WIDTH))
            raw = jnp.where(allowed, jnp.exp(scores), 0.0)
            probs = (raw * (1.0 / jnp.sum(raw, axis=1, keepdims=True))).astype(bf16)
            mixed.append(dot(probs, values).astype(bf16))
    attended = jnp.concatenate(mixed, axis=1)
    lows = merged(dot_nt(stack(2), attended), masks, rank)
    share(index_ref, attended, out_w, lows, *terms)


def share(index_ref, values, weight, lows, keep, *sends):
    rows, width = values.shape[0], sends[0].shape[1]
    half = len(sends) // 2
    left, right = slice(0, width), slice(width, 2 * width)
    for rel, at in ((1, 0), (3, half)):
        term = dot(values, weight[:, part_of(index_ref, rel, width)]).astype(bf16)
        row = 0
        for target in sends[at : at + half]:
            count = min(target.shape[0], rows - row)
            target[0:count, :] = term[row : row + count, :]
            row += count
    sends[half - 1][-lows.shape[0] :, 0:rows] = lows.astype(bf16)
    for rel, at in ((0, left), (2, right)):
        keep[0:rows, at] = dot(values, weight[:, part_of(index_ref, rel, width)])
    keep[rows:, 0:rows] = lows


def add_pair(kept, *refs):
    *arrived, _, out = refs
    half = len(arrived) // 2
    width = out.shape[1] // 2
    for at, pieces in ((slice(0, width), arrived[:half]), (slice(width, 2 * width), arrived[half:])):
        row = 0
        for piece in pieces:
            here = slice(row, row + piece.shape[0])
            out[here, at] = (kept[here, at] + piece[...].astype(f32)).astype(bf16)
            row += piece.shape[0]


def residual(chunk, lens_ref, chip, arrived, own, across, table, table_across, after, touched, out):
    rows = out.shape[0]
    width = own.shape[1]
    wanted = lens_ref.shape[1]
    rank = table.shape[0] // wanted
    here = slice(chunk * rows, (chunk + 1) * rows)
    left, right = slice(0, width), slice(width, 2 * width)
    masks = lane_masks(lens_ref, wanted, chunk * rows, rows)
    lows = chip[rows : rows + rank, 0:rows].astype(f32) + arrived[rows : rows + rank, 0:rows].astype(f32)
    lows = spread(lows.astype(bf16).astype(f32), masks)
    for mine, theirs, tokens, b in (
        (left, right, own, table),
        (right, left, across, table_across),
    ):
        total = chip[0:rows, mine].astype(f32) + arrived[0:rows, theirs].astype(f32)
        total = total + dot_tn(lows, b[...]).astype(bf16).astype(f32)
        out[:, mine] = (total + tokens[here, :].astype(f32)).astype(bf16)


def choose_second(me_ref, want_ref, *refs):
    outs = refs[-5:]
    *packed, passed = refs[:-5]
    unit = passed.shape[2]
    wanted = want_ref.shape[1]

    def use(slot, block):
        row = 0
        for out in outs:
            height = out.shape[0] // wanted
            for k in range(out.shape[1] // unit):
                out[rows_of(slot, height), k * unit : (k + 1) * unit] = block[row : row + height, :]
                row += height

    each_asked(me_ref, want_ref, packed, passed, use)


def feed_forward(
    chunk,
    index_ref, lens_ref, mine, theirs, table0, table1, table2, table3, stack_a, stack_g, stack_u, gain,
    gate_w, up_w, down_w,
    *rest,
):
    *terms, normed, hidden = rest
    rows = mine.shape[0]
    width = mine.shape[1] // 2
    wanted = lens_ref.shape[1]
    low, rank = table0.shape[0] // wanted, stack_a.shape[0] // wanted
    unit = math.gcd(width, hidden.shape[1])
    pieces = [pl.ds(k * unit, unit) for k in range(hidden.shape[1] // unit)]
    masks = lane_masks(lens_ref, wanted, chunk * rows, rows)
    loads = [
        lambda ref=ref, at=at: ref[:, at * width : (at + 1) * width].astype(f32)
        for ref, at in ((mine, 0), (theirs, 0), (mine, 1), (theirs, 1))
    ]
    normalize(index_ref, loads, gain, normed)
    products = sum(
        dot_nt(table[...], normed[:, part_of(index_ref, rel, width)])
        for rel, table in enumerate((table0, table1, table2, table3))
    )
    total = merged(products, masks, low).astype(bf16).astype(f32)
    low_gate, low_up = spread(total[0:rank], masks), spread(total[rank:], masks)
    for piece in pieces:
        gate = dot(normed[...], gate_w[:, piece])
        gate = gate + dot_tn(low_gate, stack_g[:, piece]).astype(bf16).astype(f32)
        upward = dot(normed[...], up_w[:, piece])
        upward = upward + dot_tn(low_up, stack_u[:, piece]).astype(bf16).astype(f32)
        hidden[:, piece] = (gate / (1.0 + jnp.exp(-gate)) * upward).astype(bf16)
    lows = merged(dot_nt(stack_a[...], hidden[...]), masks, rank)
    share(index_ref, hidden[...], down_w, lows, *terms)


def split_pair(rank, kept, *refs):
    *arrived, stay, away = refs
    half = len(arrived) // 2
    width = away.shape[1]
    row = 0
    for piece in arrived[:half]:
        here = slice(row, row + piece.shape[0])
        stay[here, :] = kept[here, 0:width] + piece[...].astype(f32)
        row += piece.shape[0]
    row = 0
    for piece in arrived[half:]:
        here = slice(row, row + piece.shape[0])
        away[here, :] = (kept[here, width:] + piece[...].astype(f32)).astype(bf16)
        row += piece.shape[0]
    away[row:, :] = stay[row:, :].astype(bf16)


def finish(count, lens_ref, table, *refs):
    out = refs[-1]
    wanted = lens_ref.shape[1]
    width = out.shape[1]
    for c in range(count):
        stay, arrived, resid = refs[3 * c : 3 * c + 3]
        rows = resid.shape[0]
        masks = lane_masks(lens_ref, wanted, c * rows, rows)
        lows = stay[rows:, 0:rows] + arrived[rows:, 0:rows].astype(f32)
        total = stay[0:rows, :] + arrived[0:rows, :].astype(f32)
        total = total + delta(lows.astype(bf16).astype(f32), masks, table[...])
        out[c * rows : (c + 1) * rows, :] = (total + resid[:, 0:width].astype(f32)).astype(bf16)


def rotation_tables(lens, row_count):
    half = HEAD_WIDTH // 2
    inverse = rope_base ** (-(jnp.arange(half, dtype=f32) * 2.0) / HEAD_WIDTH)
    row = jnp.arange(row_count, dtype=jnp.int32)
    start_of = jnp.zeros_like(row)
    start = jnp.int32(0)
    for j in range(lens.shape[0]):
        start_of = jnp.where(row >= start, start, start_of)
        start = start + lens[j]
    angle = (row - start_of).astype(f32)[:, None] * jnp.concatenate([inverse, inverse])[None, :]
    sign = jnp.concatenate([-jnp.ones(half, f32), jnp.ones(half, f32)])
    return jnp.cos(angle), jnp.sin(angle) * sign[None, :]


def swap_core(values):
    return lax.ppermute(values, "tp", [(k, k ^ 1) for k in range(4)])


def swap_across(values):
    return lax.ppermute(values, "tp", [(k, k ^ 2) for k in range(4)])


def swap_diagonal(values):
    return lax.ppermute(values, "tp", [(k, k ^ 3) for k in range(4)])


def swap_req(values, flips):
    return lax.ppermute(values, "req", [(k, k ^ flips) for k in range(lax.axis_size("req"))])


def per_device(
    tokens,
    lengths,
    request_adapter_index,
    attention_norm_gain,
    query_norm_gain,
    key_norm_gain,
    feedforward_norm_gain,
    query_weight,
    key_weight,
    value_weight,
    output_weight,
    gate_weight,
    up_weight,
    down_weight,
    query_key_value_adapter_input,
    output_adapter_input,
    gate_up_adapter_input,
    down_adapter_input,
    query_adapter_output,
    key_adapter_output,
    value_adapter_output,
    projection_adapter_output,
    gate_adapter_output,
    up_adapter_output,
    down_adapter_output,
):
    assert lax.axis_size("tp") == 4
    row_count, width = tokens.shape
    groups = lax.axis_size("req")
    wanted = lengths.shape[1]
    held, low_qkv, _ = query_key_value_adapter_input.shape
    rank = output_adapter_input.shape[1]
    low_gu = gate_up_adapter_input.shape[1]
    q_width, k_width = query_weight.shape[1], key_weight.shape[1]
    hidden_width = gate_weight.shape[1]
    heads, kv_heads = q_width // HEAD_WIDTH, k_width // HEAD_WIDTH
    unit = math.gcd(width, hidden_width)
    rows = row_count // CHUNKS
    assert width == q_width == 2 * k_width and rows <= width
    index = lax.axis_index("tp").astype(jnp.int32).reshape(1)
    me = lax.axis_index("req").astype(jnp.int32).reshape(1)
    want = request_adapter_index

    peers = groups // 2
    across = swap_across(tokens)
    core = swap_core(tokens)
    diagonal = swap_core(across)
    want_neighbour = swap_req(want, 1)

    def spread_out(block, *after):
        everyone = [block] + [swap_req(block, 2 * rel) for rel in range(1, peers)]
        passing = call(
            pick_for_neighbour, [SMEM] * 2 + [VMEM] * peers + [ANY] * len(after),
            shaped((peers,) + block.shape[1:], bf16),
        )(me, want_neighbour, *everyone, *after)
        return everyone, passing

    def loaded(weights, after, limit):
        return call(
            functools.partial(load, len(weights)), [ANY] * (len(weights) + len(after)),
            [shaped(w.shape, bf16) for w in weights],
            scratch=[pltpu.SemaphoreType.DMA((len(weights),))], limit=limit,
        )(*weights, *after)

    tables = (
        query_key_value_adapter_input, query_adapter_output, key_adapter_output, value_adapter_output,
        output_adapter_input, projection_adapter_output, gate_up_adapter_input, down_adapter_output,
        down_adapter_input, gate_adapter_output, up_adapter_output,
    )
    plan = (
        (0, (0, width), 0, 0),
        (1, (0, q_width), low_qkv, 0),
        (2, (0, k_width), low_qkv + rank, 0),
        (3, (0, k_width), low_qkv + rank, k_width),
        (4, (0, width), low_qkv + 2 * rank, 0),
        (5, (0, width), low_qkv + 3 * rank, 0),
    )
    plan_second, row = [], 0
    shapes = ((low_gu, width), (rank, width)) + ((rank, hidden_width),) * 3
    for table, (height, columns) in enumerate(shapes):
        for k in range(columns // unit):
            plan_second.append((6 + table, (k * unit, unit), row, 0))
            row += height
    block, block_second = call(
        functools.partial(gather_tables, (plan, tuple(plan_second))), [ANY] * len(tables),
        [shaped((held, low_qkv + 4 * rank, width), bf16), shaped((held, row, unit), bf16)],
        scratch=[pltpu.SemaphoreType.DMA((len(plan) + len(plan_second),))], limit=60,
    )(*tables)
    cosine, sine = rotation_tables(lengths[0], row_count)

    gain_one = attention_norm_gain.reshape(1, -1)
    gain_two = feedforward_norm_gain.reshape(1, -1)
    q_gain = query_norm_gain.reshape(1, -1)
    k_gain = key_norm_gain.reshape(1, -1)
    qkv_width = q_width + 2 * k_width
    normed_own, output_weight, *qkv = call(
        project_qkv, [SMEM] + [VMEM] * 5 + [ANY] * 6,
        [shaped((row_count, width), bf16), shaped(output_weight.shape, bf16)] + [shaped((rows, qkv_width), f32)] * CHUNKS,
        scratch=[
            pltpu.VMEM((row_count, 4 * width), bf16),
            pltpu.VMEM(query_weight.shape, bf16),
            pltpu.VMEM(key_weight.shape, bf16),
            pltpu.VMEM(value_weight.shape, bf16),
            pltpu.SemaphoreType.DMA((4,)),
        ],
        limit=50,
    )(
        index, tokens, core, across, diagonal, gain_one, query_weight, key_weight, value_weight,
        output_weight, cosine, sine,
    )
    everyone, passing = spread_out(block, normed_own)
    passed = swap_req(passing, 1)
    block_second = call(hold, [VMEM, ANY], shaped(block_second.shape, bf16))(block_second, passing)

    low, chosen, proj = call(
        functools.partial(low_first, rank), [SMEM] * 3 + [VMEM] * (peers + 2),
        [
            shaped((low_qkv, row_count), bf16),
            shaped((wanted, 3 * rank, width), bf16),
            shaped((wanted * rank, width), bf16),
        ],
        scratch=[pltpu.VMEM((wanted * low_qkv, width), bf16)],
    )(me, want, lengths, *everyone, passed, normed_own)
    lows = (low, swap_core(low), swap_across(low), swap_diagonal(low))
    proj_across = swap_across(proj)

    everyone, passing_second = spread_out(block_second, low)
    passed = swap_req(passing_second, 1)
    table, down_b, down_a, gate_b, up_b = call(
        choose_second, [SMEM] * 2 + [VMEM] * (peers + 1),
        [shaped((wanted * height, columns), bf16) for height, columns in shapes],
    )(me, want, *everyone, passed)
    table_across = swap_across(table)
    tables = (table, swap_core(table), table_across, swap_core(table_across))

    tall = rows + rank
    cuts = [rows // 2, rows // 2 + rank, rows // 2, rows // 2]
    terms = [shaped((tall, 2 * width), f32)] + [shaped((cut, width), bf16) for cut in cuts]
    past = [jnp.zeros((16, k_width), bf16)] * 2
    after = low
    chips = []
    for c in range(CHUNKS):
        new_k, new_v, keep, *sends = call(
            functools.partial(attend, c, heads, kv_heads),
            [SMEM] * 2 + [VMEM] * 13 + [ANY],
            [shaped((rows, k_width), bf16)] * 2 + terms,
        )(
            index, lengths, qkv[c], *lows, chosen, cosine, sine,
            q_gain, k_gain, output_weight, *past, after,
        )
        past = [new_k, new_v] if c == 0 else [
            jnp.concatenate([old, new], axis=0) for old, new in zip(past, (new_k, new_v))
        ]
        after = call(add_pair, [VMEM] * 5 + [ANY], shaped((tall, 2 * width), bf16))(
            keep, *[swap_core(piece) for piece in sends], passing_second
        )
        chips.append(after)

    gate_weight, up_weight, down_weight = loaded(
        (gate_weight, up_weight, down_weight), (after,), 44
    )
    ends = []
    for c in range(CHUNKS):
        resid = call(
            functools.partial(residual, c), [SMEM] + [VMEM] * 6 + [ANY] * 2,
            shaped((rows, 2 * width), bf16),
        )(lengths, chips[c], swap_across(chips[c]), tokens, across, proj, proj_across, after,
          gate_weight)
        keep, *sends = call(
            functools.partial(feed_forward, c),
            [SMEM] * 2 + [VMEM] * 13,
            terms,
            limit=32,
            scratch=[
                pltpu.VMEM((rows, 4 * width), bf16),
                pltpu.VMEM((rows, hidden_width), bf16),
            ],
        )(
            index, lengths, resid, swap_core(resid), *tables, down_a, gate_b, up_b,
            gain_two, gate_weight, up_weight, down_weight,
        )
        stay, away = call(
            functools.partial(split_pair, rank), [VMEM] * 5,
            [shaped((tall, width), f32), shaped((tall, width), bf16)],
        )(keep, *[swap_core(piece) for piece in sends])
        after = away
        ends += [stay, swap_across(away), resid]
    return call(
        functools.partial(finish, CHUNKS), [SMEM] + [VMEM] * (1 + 3 * CHUNKS),
        shaped((row_count, width), bf16),
    )(lengths, down_b, *ends)


def solution(mesh):
    placed = (
        P("req", "tp"),
        P("req", None),
        P("req", None),
        P(),
        P(),
        P(),
        P(),
        P(None, "tp"),
        P(None, "tp"),
        P(None, "tp"),
        P("tp", None),
        P(None, "tp"),
        P(None, "tp"),
        P("tp", None),
        P("req", None, "tp"),
        P("req", None, "tp"),
        P("req", None, "tp"),
        P("req", None, "tp"),
        P("req", None, "tp"),
        P("req", None, "tp"),
        P("req", None, "tp"),
        P("req", None, "tp"),
        P("req", None, "tp"),
        P("req", None, "tp"),
        P("req", None, "tp"),
    )
    return jax.shard_map(
        per_device, mesh=mesh, in_specs=placed, out_specs=P("req", "tp"), check_vma=False
    )
```

```python
import functools
import math

import jax
import jax.numpy as jnp
from jax import lax
from jax.experimental import pallas as pl
from jax.experimental.pallas import tpu as pltpu
from jax.sharding import PartitionSpec as P

HEAD_WIDTH = 128
CHUNKS = 2

epsilon = 1e-06
rope_base = 1000000.0

bf16 = jnp.bfloat16
f32 = jnp.float32
VMEM = pl.BlockSpec(memory_space=pltpu.VMEM)
ANY = pl.BlockSpec(memory_space=pl.ANY)
HBM = pl.BlockSpec(memory_space=pltpu.HBM)
SMEM = pl.BlockSpec(memory_space=pltpu.SMEM)


def call(body, in_specs, outs, scratch=(), limit=16, out_specs=None):
    single = not isinstance(outs, (list, tuple))
    if out_specs is None:
        out_specs = VMEM if single else [VMEM] * len(outs)
    return pl.pallas_call(
        body,
        out_shape=outs if single else list(outs),
        in_specs=in_specs,
        out_specs=out_specs,
        scratch_shapes=list(scratch),
        compiler_params=pltpu.CompilerParams(vmem_limit_bytes=limit * 1024 * 1024),
        cost_estimate=pl.CostEstimate(flops=1, bytes_accessed=1, transcendentals=0),
    )


def shaped(shape, dtype):
    return jax.ShapeDtypeStruct(shape, dtype)


def dot(a, b):
    return lax.dot_general(a, b, (((1,), (0,)), ((), ())), preferred_element_type=f32)


def dot_nt(a, b):
    return lax.dot_general(a, b, (((1,), (1,)), ((), ())), preferred_element_type=f32)


def dot_tn(a, b):
    return lax.dot_general(a, b, (((0,), (0,)), ((), ())), preferred_element_type=f32)


def part_of(index_ref, rel, width):
    return pl.ds(pl.multiple_of((index_ref[0] ^ rel) * width, width), width)


def bounds(lens_ref, count):
    starts, total = [], jnp.int32(0)
    for j in range(count):
        starts.append(total)
        total = total + lens_ref[0, j]
    return starts, starts[1:] + [total]


def lane_masks(lens_ref, count, first, width):
    starts, ends = bounds(lens_ref, count)
    rows = lax.broadcasted_iota(jnp.int32, (1, width), 1) + first
    return [((rows >= s) & (rows < e)).astype(f32) for s, e in zip(starts, ends)]


def spread(piece, masks):
    return jnp.concatenate([piece * m for m in masks], axis=0).astype(bf16)


def merged(products, masks, low):
    return sum(products[j * low : (j + 1) * low, :] * m for j, m in enumerate(masks))


def delta(piece, masks, stack):
    return dot_tn(spread(piece, masks), stack).astype(bf16).astype(f32)


def start_all(pairs, sems):
    copies = [pltpu.make_async_copy(a, b, sems.at[k]) for k, (a, b) in enumerate(pairs)]
    for copy in copies:
        copy.start()
    return copies


def gather_tables(plans, *refs):
    *refs, sems = refs
    pairs = []
    for plan, out in zip(plans, refs[-len(plans) :]):
        for table, columns, row, column in plan:
            source = refs[table]
            there = out.at[:, pl.ds(row, source.shape[1]), pl.ds(column, columns[1])]
            pairs.append((source.at[:, :, pl.ds(*columns)], there))
    for copy in start_all(pairs, sems):
        copy.wait()


def load(count, *refs):
    for copy in start_all(list(zip(refs[:count], refs[-1 - count : -1])), refs[-1]):
        copy.wait()


def owner_at(me_ref, rel, flip):
    return me_ref[0] ^ (2 * rel + flip)


def pick_for_neighbour(me_ref, want_ref, *refs):
    *packed, _, _, send = refs
    held = packed[0].shape[-3]
    for rel in range(send.shape[0]):
        owner = owner_at(me_ref, rel, 0)
        ref = packed[rel]
        pick = jnp.int32(0)
        for j in range(want_ref.shape[1]):
            a = want_ref[0, j]
            pick = pick + jnp.where(a // held == owner, a % held, 0)
        send[rel] = ref[pick]


def hold(block, after, out):
    out[...] = block[...]


def each_asked(me_ref, want_ref, packed, passed, use):
    held = packed[0].shape[-3]
    for rel in range(passed.shape[0]):
        for flip in range(2):
            owner = owner_at(me_ref, rel, flip)
            slot, pick, found = jnp.int32(0), jnp.int32(0), jnp.int32(0)
            for j in range(want_ref.shape[1]):
                a = want_ref[0, j]
                hit = (a // held == owner).astype(jnp.int32)
                slot, pick, found = slot + hit * j, pick + hit * (a % held), found + hit

            @pl.when(found > 0)
            def _():
                use(slot, passed.at[rel] if flip else packed[rel].at[pick])


def normalize(index_ref, refs, gain, normed, keep_own=None):
    blocks = [load() for load in refs]
    width = blocks[0].shape[1]
    square = sum(jnp.sum(b * b, axis=1, keepdims=True) for b in blocks)
    scale = lax.rsqrt(square / (len(blocks) * width) + epsilon)
    for rel, block in enumerate(blocks):
        part = part_of(index_ref, rel, width)
        value = (block * scale * gain[:, part]).astype(bf16)
        normed[:, part] = value
        if rel == 0 and keep_own is not None:
            keep_own(value)


def project_qkv(
    index_ref, own, core, across, diagonal, gain, q_hbm, k_hbm, v_hbm,
    normed_own, *rest,
):
    *outs, normed, q_w, k_w, v_w, sems = rest
    copies = start_all([(q_hbm, q_w), (k_hbm, k_w), (v_hbm, v_w)], sems)
    rows = own.shape[0] // len(outs)
    q_width, k_width = q_w.shape[1], k_w.shape[1]
    for c in range(len(outs)):
        here = slice(c * rows, (c + 1) * rows)

        def keep_own(value):
            normed_own[here, :] = value

        loads = [lambda ref=ref: ref[here, :].astype(f32) for ref in (own, core, across, diagonal)]
        normalize(index_ref, loads, gain, normed.at[here, :], keep_own)
    for w, copy, low, high in (
        (q_w, copies[0], 0, q_width),
        (k_w, copies[1], q_width, q_width + k_width),
        (v_w, copies[2], q_width + k_width, q_width + 2 * k_width),
    ):
        copy.wait()
        for c, out in enumerate(outs):
            out[:, low:high] = dot(normed[c * rows : (c + 1) * rows, :], w[...])


def rows_of(slot, height):
    return pl.ds(pl.multiple_of(slot * height, 16), height)


def low_first(rank, me_ref, want_ref, lens_ref, *refs):
    *packed, passed, normed_own, _, _, _, out, chosen, both, stack = refs
    wanted = want_ref.shape[1]
    low = out.shape[0]

    def use(slot, block):
        stack[rows_of(slot, low), :] = block[0:low, :]
        chosen[slot] = block[low : low + 3 * rank, :]
        at = pl.ds(pl.multiple_of(low + slot * rank, 16), rank)
        both[at, :] = block[low + 3 * rank :, :]

    each_asked(me_ref, want_ref, packed, passed, use)
    products = dot_nt(stack[...], normed_own[...])
    masks = lane_masks(lens_ref, wanted, 0, normed_own.shape[0])
    value = merged(products, masks, low).astype(bf16)
    out[...] = value
    both[0:low, :] = value


def attend(
    chunk, heads, kv_heads,
    index_ref, lens_ref, qkv, low0, low1, low2, low3, chosen, cosine, sine,
    q_gain, k_gain, out_w, old_k, old_v, after,
    new_k, new_v, *terms,
):
    rows = qkv.shape[0]
    width = out_w.shape[0]
    first = chunk * rows
    here = slice(first, first + rows)
    wanted, rank = chosen.shape[0], chosen.shape[1] // 3
    q_width, k_width = heads * HEAD_WIDTH, kv_heads * HEAD_WIDTH

    def stack(number, columns=slice(None)):
        block = chosen[:, number * rank : (number + 1) * rank, columns]
        return block.reshape(wanted * rank, block.shape[2])

    masks = lane_masks(lens_ref, wanted, first, rows)
    low = low0.shape[0]
    total = sum(ref[0:low, here].astype(f32) for ref in (low0, low1, low2, low3))
    total = total.astype(bf16).astype(f32)
    query = qkv[:, 0:q_width] + delta(total[0:rank], masks, stack(0))
    key = qkv[:, q_width : q_width + k_width] + delta(total[rank : 2 * rank], masks, stack(1, slice(0, k_width)))
    value = qkv[:, q_width + k_width :] + delta(total[2 * rank :], masks, stack(1, slice(k_width, 2 * k_width)))
    new_v[...] = value.astype(bf16)
    cos, sin = cosine[here, :], sine[here, :]

    def turn(values, gain):
        square = jnp.mean(values * values, axis=1, keepdims=True)
        values = values * lax.rsqrt(square + epsilon) * gain[...]
        return (values * cos + pltpu.roll(values, HEAD_WIDTH // 2, 1) * sin).astype(bf16)

    def head(h):
        return slice(h * HEAD_WIDTH, (h + 1) * HEAD_WIDTH)

    for h in range(kv_heads):
        new_k[:, head(h)] = turn(key[:, head(h)], k_gain)
    seen = first + rows
    starts, _ = bounds(lens_ref, wanted)
    down = lax.broadcasted_iota(jnp.int32, (rows, 1), 0) + first
    start_of = jnp.zeros((rows, 1), jnp.int32)
    for s in starts:
        start_of = jnp.where(down >= s, s, start_of)
    along = lax.broadcasted_iota(jnp.int32, (rows, seen), 1)
    allowed = (along <= down) & (along >= start_of)
    group = heads // kv_heads
    mixed = []
    for kv in range(kv_heads):
        keys, values = new_k[:, head(kv)], new_v[:, head(kv)]
        if chunk > 0:
            keys = jnp.concatenate([old_k[:, head(kv)], keys], axis=0)
            values = jnp.concatenate([old_v[:, head(kv)], values], axis=0)
        for h in range(kv * group, (kv + 1) * group):
            scores = dot_nt(turn(query[:, head(h)], q_gain), keys) * (1.0 / math.sqrt(HEAD_WIDTH))
            raw = jnp.where(allowed, jnp.exp(scores), 0.0)
            probs = (raw * (1.0 / jnp.sum(raw, axis=1, keepdims=True))).astype(bf16)
            mixed.append(dot(probs, values).astype(bf16))
    attended = jnp.concatenate(mixed, axis=1)
    lows = merged(dot_nt(stack(2), attended), masks, rank)
    share(index_ref, attended, out_w, lows, *terms)


def share(index_ref, values, weight, lows, keep, *sends):
    rows, width = values.shape[0], sends[0].shape[1]
    half = len(sends) // 2
    left, right = slice(0, width), slice(width, 2 * width)
    for rel, at in ((1, 0), (3, half)):
        term = dot(values, weight[:, part_of(index_ref, rel, width)]).astype(bf16)
        row = 0
        for target in sends[at : at + half]:
            count = min(target.shape[0], rows - row)
            target[0:count, :] = term[row : row + count, :]
            row += count
    sends[half - 1][-lows.shape[0] :, 0:rows] = lows.astype(bf16)
    for rel, at in ((0, left), (2, right)):
        keep[0:rows, at] = dot(values, weight[:, part_of(index_ref, rel, width)])
    keep[rows:, 0:rows] = lows


def add_pair(kept, *refs):
    *arrived, _, _, out = refs
    half = len(arrived) // 2
    width = out.shape[1] // 2
    for at, pieces in ((slice(0, width), arrived[:half]), (slice(width, 2 * width), arrived[half:])):
        row = 0
        for piece in pieces:
            here = slice(row, row + piece.shape[0])
            out[here, at] = (kept[here, at] + piece[...].astype(f32)).astype(bf16)
            row += piece.shape[0]


def residual(chunk, lens_ref, chip, arrived, own, across, table, table_across, after, touched, *outs):
    half, width = outs[0].shape
    rows = 2 * half
    wanted = lens_ref.shape[1]
    rank = chip.shape[0] - rows
    low = table.shape[0] - wanted * rank
    left, right = slice(0, width), slice(width, 2 * width)
    masks = lane_masks(lens_ref, wanted, chunk * rows, rows)
    lows = chip[rows : rows + rank, 0:rows].astype(f32) + arrived[rows : rows + rank, 0:rows].astype(f32)
    lows = spread(lows.astype(bf16).astype(f32), masks)
    for number, (mine, theirs, tokens, b) in enumerate(
        ((left, right, own, table), (right, left, across, table_across))
    ):
        total = chip[0:rows, mine].astype(f32) + arrived[0:rows, theirs].astype(f32)
        total = total + dot_tn(lows, b[low:, :]).astype(bf16).astype(f32)
        total = (total + tokens[chunk * rows : (chunk + 1) * rows, :].astype(f32)).astype(bf16)
        outs[2 * number][...] = total[:half]
        outs[2 * number + 1][...] = total[half:]


def choose_second(me_ref, want_ref, *refs):
    *packed, passed, _ = refs[:-5]
    outs = refs[-5:]
    unit = passed.shape[2]
    wanted = want_ref.shape[1]

    def use(slot, block):
        row = 0
        for out in outs:
            height = out.shape[0] // wanted
            for k in range(out.shape[1] // unit):
                out[rows_of(slot, height), k * unit : (k + 1) * unit] = block[row : row + height, :]
                row += height

    each_asked(me_ref, want_ref, packed, passed, use)


def feed_forward(
    chunk,
    index_ref, lens_ref, left0, left1, right0, right1, left2, left3, right2, right3,
    table0, table1, table2, table3, stack_a, stack_g, stack_u, gain, gate_w, up_w, down_w,
    *rest,
):
    *terms, normed, hidden = rest
    half, width = left0.shape
    rows = 2 * half
    wanted = lens_ref.shape[1]
    low, rank = table0.shape[0] // wanted, stack_a.shape[0] // wanted
    unit = math.gcd(width, hidden.shape[1])
    pieces = [pl.ds(k * unit, unit) for k in range(hidden.shape[1] // unit)]
    masks = lane_masks(lens_ref, wanted, chunk * rows, rows)
    for k, refs in enumerate(((left0, left2, right0, right2), (left1, left3, right1, right3))):
        loads = [lambda ref=ref: ref[...].astype(f32) for ref in refs]
        normalize(index_ref, loads, gain, normed.at[k * half : (k + 1) * half, :])
    products = sum(
        dot_nt(table[...], normed[:, part_of(index_ref, rel, width)])
        for rel, table in enumerate((table0, table1, table2, table3))
    )
    total = merged(products, masks, low).astype(bf16).astype(f32)
    low_gate, low_up = spread(total[0:rank], masks), spread(total[rank:], masks)
    for piece in pieces:
        gate = dot(normed[...], gate_w[:, piece])
        gate = gate + dot_tn(low_gate, stack_g[:, piece]).astype(bf16).astype(f32)
        upward = dot(normed[...], up_w[:, piece])
        upward = upward + dot_tn(low_up, stack_u[:, piece]).astype(bf16).astype(f32)
        hidden[:, piece] = (gate / (1.0 + jnp.exp(-gate)) * upward).astype(bf16)
    lows = merged(dot_nt(stack_a[...], hidden[...]), masks, rank)
    share(index_ref, hidden[...], down_w, lows, *terms)


def split_pair(rank, kept, *refs):
    *arrived, _, stay, away = refs
    half = len(arrived) // 2
    width = away.shape[1]
    row = 0
    for piece in arrived[:half]:
        here = slice(row, row + piece.shape[0])
        stay[here, :] = kept[here, 0:width] + piece[...].astype(f32)
        row += piece.shape[0]
    row = 0
    for piece in arrived[half:]:
        here = slice(row, row + piece.shape[0])
        away[here, :] = (kept[here, width:] + piece[...].astype(f32)).astype(bf16)
        row += piece.shape[0]
    away[row:, :] = stay[row:, :].astype(bf16)


def finish(count, lens_ref, table, *refs):
    out = refs[-1]
    wanted = lens_ref.shape[1]
    width = out.shape[1]
    for c in range(count):
        stay, arrived, *resid = refs[4 * c : 4 * c + 4]
        half = resid[0].shape[0]
        rows = 2 * half
        masks = lane_masks(lens_ref, wanted, c * rows, rows)
        lows = stay[rows:, 0:rows] + arrived[rows:, 0:rows].astype(f32)
        total = stay[0:rows, :] + arrived[0:rows, :].astype(f32)
        total = total + delta(lows.astype(bf16).astype(f32), masks, table[...])
        for k, piece in enumerate(resid):
            at = slice(k * half, (k + 1) * half)
            out[c * rows + k * half : c * rows + (k + 1) * half, :] = (
                total[at, :] + piece[...].astype(f32)
            ).astype(bf16)


def rotation_tables(lens, row_count):
    half = HEAD_WIDTH // 2
    inverse = rope_base ** (-(jnp.arange(half, dtype=f32) * 2.0) / HEAD_WIDTH)
    row = jnp.arange(row_count, dtype=jnp.int32)
    start_of = jnp.zeros_like(row)
    start = jnp.int32(0)
    for j in range(lens.shape[0]):
        start_of = jnp.where(row >= start, start, start_of)
        start = start + lens[j]
    angle = (row - start_of).astype(f32)[:, None] * jnp.concatenate([inverse, inverse])[None, :]
    sign = jnp.concatenate([-jnp.ones(half, f32), jnp.ones(half, f32)])
    return jnp.cos(angle), jnp.sin(angle) * sign[None, :]


def swap_core(values):
    return lax.ppermute(values, "tp", [(k, k ^ 1) for k in range(4)])


def swap_across(values):
    return lax.ppermute(values, "tp", [(k, k ^ 2) for k in range(4)])


def swap_diagonal(values):
    return lax.ppermute(values, "tp", [(k, k ^ 3) for k in range(4)])


def swap_req(values, flips):
    return lax.ppermute(values, "req", [(k, k ^ flips) for k in range(lax.axis_size("req"))])


def per_device(
    tokens,
    lengths,
    request_adapter_index,
    attention_norm_gain,
    query_norm_gain,
    key_norm_gain,
    feedforward_norm_gain,
    query_weight,
    key_weight,
    value_weight,
    output_weight,
    gate_weight,
    up_weight,
    down_weight,
    query_key_value_adapter_input,
    output_adapter_input,
    gate_up_adapter_input,
    down_adapter_input,
    query_adapter_output,
    key_adapter_output,
    value_adapter_output,
    projection_adapter_output,
    gate_adapter_output,
    up_adapter_output,
    down_adapter_output,
):
    assert lax.axis_size("tp") == 4
    row_count, width = tokens.shape
    groups = lax.axis_size("req")
    wanted = lengths.shape[1]
    held, low_qkv, _ = query_key_value_adapter_input.shape
    rank = output_adapter_input.shape[1]
    low_gu = gate_up_adapter_input.shape[1]
    q_width, k_width = query_weight.shape[1], key_weight.shape[1]
    hidden_width = gate_weight.shape[1]
    heads, kv_heads = q_width // HEAD_WIDTH, k_width // HEAD_WIDTH
    unit = math.gcd(width, hidden_width)
    rows = row_count // CHUNKS
    assert width == q_width == 2 * k_width == row_count
    index = lax.axis_index("tp").astype(jnp.int32).reshape(1)
    me = lax.axis_index("req").astype(jnp.int32).reshape(1)
    want = request_adapter_index

    peers = groups // 2
    across = swap_across(tokens)
    core = swap_core(tokens)
    diagonal = swap_diagonal(tokens)
    want_neighbour = swap_req(want, 1)

    def for_neighbour(blocks, *after):
        return call(
            pick_for_neighbour, [SMEM] * 2 + [VMEM] * len(blocks) + [ANY] * 2,
            shaped((peers,) + blocks[0].shape[-2:], bf16),
        )(me, want_neighbour, *blocks, *after)

    def loaded(weights, after, limit):
        return call(
            functools.partial(load, len(weights)), [ANY] * (len(weights) + len(after)),
            [shaped(w.shape, bf16) for w in weights],
            scratch=[pltpu.SemaphoreType.DMA((len(weights),))], limit=limit,
        )(*weights, *after)

    tables = (
        query_key_value_adapter_input, query_adapter_output, key_adapter_output, value_adapter_output,
        output_adapter_input, projection_adapter_output, gate_up_adapter_input, down_adapter_output,
        down_adapter_input, gate_adapter_output, up_adapter_output,
    )
    plan = (
        (0, (0, width), 0, 0),
        (1, (0, q_width), low_qkv, 0),
        (2, (0, k_width), low_qkv + rank, 0),
        (3, (0, k_width), low_qkv + rank, k_width),
        (4, (0, width), low_qkv + 2 * rank, 0),
        (5, (0, width), low_qkv + 3 * rank, 0),
    )
    plan_second, row = [], 0
    shapes = ((low_gu, width), (rank, width)) + ((rank, hidden_width),) * 3
    for table, (height, columns) in enumerate(shapes):
        for k in range(columns // unit):
            plan_second.append((6 + table, (k * unit, unit), row, 0))
            row += height
    block, block_second = call(
        functools.partial(gather_tables, (plan, tuple(plan_second))), [ANY] * len(tables),
        [shaped((held, low_qkv + 4 * rank, width), bf16), shaped((held, row, unit), bf16)],
        scratch=[pltpu.SemaphoreType.DMA((len(plan) + len(plan_second),))], limit=60,
    )(*tables)
    cosine, sine = rotation_tables(lengths[0], row_count)

    gain_one = attention_norm_gain.reshape(1, -1)
    gain_two = feedforward_norm_gain.reshape(1, -1)
    q_gain = query_norm_gain.reshape(1, -1)
    k_gain = key_norm_gain.reshape(1, -1)
    qkv_width = q_width + 2 * k_width
    normed_own, *qkv = call(
        project_qkv, [SMEM] + [VMEM] * 5 + [HBM] * 3,
        [shaped((row_count, width), bf16)] + [shaped((rows, qkv_width), f32)] * CHUNKS,
        scratch=[
            pltpu.VMEM((row_count, 4 * width), bf16),
            pltpu.VMEM(query_weight.shape, bf16),
            pltpu.VMEM(key_weight.shape, bf16),
            pltpu.VMEM(value_weight.shape, bf16),
            pltpu.SemaphoreType.DMA((3,)),
        ],
        limit=50,
    )(
        index, tokens, core, across, diagonal, gain_one, query_weight, key_weight, value_weight,
    )
    everyone = [block] + [swap_req(block, 2 * rel) for rel in range(1, peers)]
    passing = for_neighbour(everyone, cosine, sine)
    block_second = call(hold, [VMEM, ANY], shaped(block_second.shape, bf16))(block_second, passing)
    second = [block_second] + [swap_req(block_second, 2 * rel) for rel in range(1, peers)]
    (output_weight,) = loaded((output_weight,), (passing,), 48)
    low, chosen, low_proj = call(
        functools.partial(low_first, rank), [SMEM] * 3 + [VMEM] * (peers + 2) + [ANY] * 3,
        [
            shaped((low_qkv, row_count), bf16),
            shaped((wanted, 3 * rank, width), bf16),
            shaped((low_qkv + wanted * rank, width), bf16),
        ],
        scratch=[pltpu.VMEM((wanted * low_qkv, width), bf16)],
    )(
        me, want, lengths, *everyone, swap_req(passing, 1), normed_own,
        cosine, sine, output_weight,
    )
    low_proj_across = swap_across(low_proj)
    lows = (low, swap_core(low), low_proj_across, swap_diagonal(low))

    tall = rows + rank
    cuts = [rows // 2, rows // 2 + rank, rows // 2, rows // 2]
    terms = [shaped((tall, 2 * width), f32)] + [shaped((cut, width), bf16) for cut in cuts]
    past = [jnp.zeros((16, k_width), bf16)] * 2
    after = low
    residuals = []
    for c in range(CHUNKS):
        new_k, new_v, keep, *sends = call(
            functools.partial(attend, c, heads, kv_heads),
            [SMEM] * 2 + [VMEM] * 13 + [ANY],
            [shaped((rows, k_width), bf16)] * 2 + terms,
        )(
            index, lengths, qkv[c], *lows, chosen, cosine, sine,
            q_gain, k_gain, output_weight, *past, after,
        )
        past = [new_k, new_v] if c == 0 else [
            jnp.concatenate([old, new], axis=0) for old, new in zip(past, (new_k, new_v))
        ]
        if c == 0:
            passing_second = for_neighbour(second, new_k, low)
        chip = call(add_pair, [VMEM] * 5 + [ANY] * 2, shaped((tall, 2 * width), bf16))(
            keep, *[swap_core(piece) for piece in sends], passing_second if c == 0 else residuals[-1][0],
            keep if c == 0 else table_across,
        )
        after = chip
        if c == 0:
            gate_weight, up_weight, down_weight = loaded(
                (gate_weight, up_weight, down_weight), (chip,), 44
            )
            table, down_b, down_a, gate_b, up_b = call(
                choose_second, [SMEM] * 2 + [VMEM] * (peers + 1) + [ANY],
                [shaped((wanted * height, columns), bf16) for height, columns in shapes],
            )(me, want, *second, swap_req(passing_second, 1), gate_weight)
            table_across = swap_across(table)
            tables = (table, swap_core(table), table_across, swap_core(table_across))
        resid = call(
            functools.partial(residual, c), [SMEM] + [VMEM] * 6 + [ANY] * 2,
            [shaped((rows // 2, width), bf16)] * 4,
        )(
            lengths, chip, swap_across(chip), tokens, across, low_proj, low_proj_across, new_k, table,
        )
        residuals.append(resid)

    ends = []
    arrived = gate_weight
    for c in range(CHUNKS):
        resid = residuals[c]
        keep, *sends = call(
            functools.partial(feed_forward, c),
            [SMEM] * 2 + [VMEM] * 19,
            terms,
            limit=32,
            scratch=[
                pltpu.VMEM((rows, 4 * width), bf16),
                pltpu.VMEM((rows, hidden_width), bf16),
            ],
        )(
            index, lengths, *resid, *[swap_core(piece) for piece in resid], *tables, down_a, gate_b, up_b,
            gain_two, gate_weight, up_weight, down_weight,
        )
        stay, away = call(
            functools.partial(split_pair, rank), [VMEM] * 5 + [ANY],
            [shaped((tall, width), f32), shaped((tall, width), bf16)],
        )(keep, *[swap_core(piece) for piece in sends], arrived)
        after = away
        arrived = swap_across(away)
        ends += [stay, arrived, *resid[:2]]
    return call(
        functools.partial(finish, CHUNKS), [SMEM] + [VMEM] * (1 + 4 * CHUNKS),
        shaped((row_count, width), bf16),
    )(lengths, down_b, *ends)


def solution(mesh):
    placed = (
        P("req", "tp"),
        P("req", None),
        P("req", None),
        P(),
        P(),
        P(),
        P(),
        P(None, "tp"),
        P(None, "tp"),
        P(None, "tp"),
        P("tp", None),
        P(None, "tp"),
        P(None, "tp"),
        P("tp", None),
        P("req", None, "tp"),
        P("req", None, "tp"),
        P("req", None, "tp"),
        P("req", None, "tp"),
        P("req", None, "tp"),
        P("req", None, "tp"),
        P("req", None, "tp"),
        P("req", None, "tp"),
        P("req", None, "tp"),
        P("req", None, "tp"),
        P("req", None, "tp"),
    )
    return jax.shard_map(
        per_device, mesh=mesh, in_specs=placed, out_specs=P("req", "tp"), check_vma=False
    )
```

```python
import functools
import math

import jax
import jax.numpy as jnp
from jax import lax
from jax.experimental import pallas as pl
from jax.experimental.pallas import tpu as pltpu
from jax.sharding import PartitionSpec as P

HEAD_WIDTH = 128
CHUNKS = 2

epsilon = 1e-06
rope_base = 1000000.0

bf16 = jnp.bfloat16
f32 = jnp.float32
VMEM = pl.BlockSpec(memory_space=pltpu.VMEM)
ANY = pl.BlockSpec(memory_space=pl.ANY)
HBM = pl.BlockSpec(memory_space=pltpu.HBM)
SMEM = pl.BlockSpec(memory_space=pltpu.SMEM)


def call(body, in_specs, outs, scratch=(), limit=16, out_specs=None):
    single = not isinstance(outs, (list, tuple))
    if out_specs is None:
        out_specs = VMEM if single else [VMEM] * len(outs)
    return pl.pallas_call(
        body,
        out_shape=outs if single else list(outs),
        in_specs=in_specs,
        out_specs=out_specs,
        scratch_shapes=list(scratch),
        compiler_params=pltpu.CompilerParams(vmem_limit_bytes=limit * 1024 * 1024),
        cost_estimate=pl.CostEstimate(flops=1, bytes_accessed=1, transcendentals=0),
    )


def shaped(shape, dtype):
    return jax.ShapeDtypeStruct(shape, dtype)


def dot(a, b):
    return lax.dot_general(a, b, (((1,), (0,)), ((), ())), preferred_element_type=f32)


def dot_nt(a, b):
    return lax.dot_general(a, b, (((1,), (1,)), ((), ())), preferred_element_type=f32)


def dot_tn(a, b):
    return lax.dot_general(a, b, (((0,), (0,)), ((), ())), preferred_element_type=f32)


def part_of(index_ref, rel, width):
    return pl.ds(pl.multiple_of((index_ref[0] ^ rel) * width, width), width)


def bounds(lens_ref, count):
    starts, total = [], jnp.int32(0)
    for j in range(count):
        starts.append(total)
        total = total + lens_ref[0, j]
    return starts, starts[1:] + [total]


def lane_masks(lens_ref, count, first, width):
    starts, ends = bounds(lens_ref, count)
    rows = lax.broadcasted_iota(jnp.int32, (1, width), 1) + first
    return [((rows >= s) & (rows < e)).astype(f32) for s, e in zip(starts, ends)]


def spread(piece, masks):
    return jnp.concatenate([piece * m for m in masks], axis=0).astype(bf16)


def merged(products, masks, low):
    return sum(products[j * low : (j + 1) * low, :] * m for j, m in enumerate(masks))


def delta(piece, masks, stack):
    return dot_tn(spread(piece, masks), stack).astype(bf16).astype(f32)


def start_all(pairs, sems):
    copies = [pltpu.make_async_copy(a, b, sems.at[k]) for k, (a, b) in enumerate(pairs)]
    for copy in copies:
        copy.start()
    return copies


def gather_tables(plans, *refs):
    *refs, sems = refs
    pairs = []
    for plan, out in zip(plans, refs[-len(plans) :]):
        for table, columns, row, column in plan:
            source = refs[table]
            there = out.at[:, pl.ds(row, source.shape[1]), pl.ds(column, columns[1])]
            pairs.append((source.at[:, :, pl.ds(*columns)], there))
    for copy in start_all(pairs, sems):
        copy.wait()


def load(count, *refs):
    for copy in start_all(list(zip(refs[:count], refs[-1 - count : -1])), refs[-1]):
        copy.wait()


def owner_at(me_ref, rel, flip):
    return me_ref[0] ^ (2 * rel + flip)


def pick_for_neighbour(count, me_ref, want_ref, *refs):
    packed, sends = refs[:count], refs[count + 1 :]
    held = packed[0].shape[0]
    for rel, ref in enumerate(packed):
        owner = owner_at(me_ref, rel, 0)
        pick = jnp.int32(0)
        for j in range(want_ref.shape[1]):
            a = want_ref[0, j]
            pick = pick + jnp.where(a // held == owner, a % held, 0)
        row = 0
        for send in sends:
            height = send.shape[1]
            send[rel] = ref[pick, row : row + height, :]
            row += height


def hold(block, after, out):
    out[...] = block[...]


def each_asked(me_ref, want_ref, packed, passed, use, first=0):
    held = packed[0].shape[-3]
    for rel in range(passed.shape[0]):
        for flip in range(2):
            owner = owner_at(me_ref, rel, flip)
            slot, pick, found = jnp.int32(0), jnp.int32(0), jnp.int32(0)
            for j in range(want_ref.shape[1]):
                a = want_ref[0, j]
                hit = (a // held == owner).astype(jnp.int32)
                slot, pick, found = slot + hit * j, pick + hit * (a % held), found + hit

            @pl.when(found > 0)
            def _():
                rows = pl.ds(first, passed.shape[1])
                use(slot, passed.at[rel] if flip else packed[rel].at[pick, rows, :])


def normalize(index_ref, refs, gain, normed, keep_own=None):
    blocks = [load() for load in refs]
    width = blocks[0].shape[1]
    square = sum(jnp.sum(b * b, axis=1, keepdims=True) for b in blocks)
    scale = lax.rsqrt(square / (len(blocks) * width) + epsilon)
    for rel, block in enumerate(blocks):
        part = part_of(index_ref, rel, width)
        value = (block * scale * gain[:, part]).astype(bf16)
        normed[:, part] = value
        if rel == 0 and keep_own is not None:
            keep_own(value)


def project_qkv(
    index_ref, own, core, across, diagonal, gain, q_hbm, k_hbm, v_hbm, out_hbm,
    normed_own, out_w, *rest,
):
    *outs, q_w, k_w, v_w, sems = rest
    rows, width = own.shape[0] // len(outs), own.shape[1]
    q_width, k_width = q_w.shape[1], k_w.shape[1]
    parts = [part_of(index_ref, rel, width) for rel in range(4)]
    pairs = []
    for part in parts:
        pairs += [(a.at[part, :], b.at[part, :]) for a, b in ((q_hbm, q_w), (k_hbm, k_w), (v_hbm, v_w))]
    copies = start_all(pairs + [(out_hbm, out_w)], sems)
    scales = []
    for c in range(len(outs)):
        here = slice(c * rows, (c + 1) * rows)
        square = jnp.zeros((rows, 1), f32)
        for ref in (own, core, across, diagonal):
            block = ref[here, :].astype(f32)
            square = square + jnp.sum(block * block, axis=1, keepdims=True)
        scales.append(lax.rsqrt(square / (4 * width) + epsilon))
    for rel, ref in enumerate((own, core, across, diagonal)):
        part = parts[rel]
        for copy in copies[3 * rel : 3 * rel + 3]:
            copy.wait()
        for c, out in enumerate(outs):
            here = slice(c * rows, (c + 1) * rows)
            normed = (ref[here, :].astype(f32) * scales[c] * gain[:, part]).astype(bf16)
            if rel == 0:
                normed_own[here, :] = normed
            for w, low, high in (
                (q_w, 0, q_width),
                (k_w, q_width, q_width + k_width),
                (v_w, q_width + k_width, q_width + 2 * k_width),
            ):
                term = dot(normed, w[part, :])
                if rel == 0:
                    out[:, low:high] = term
                else:
                    out[:, low:high] += term
    copies[-1].wait()


def rows_of(slot, height):
    return pl.ds(pl.multiple_of(slot * height, 16), height)


def low_first(rank, me_ref, want_ref, lens_ref, *refs):
    *packed, passed, normed_own, _, _, out, chosen, stack = refs
    wanted = want_ref.shape[1]
    low = out.shape[0]

    def use(slot, block):
        stack[rows_of(slot, low), :] = block[0:low, :]
        chosen[slot] = block[low : low + 3 * rank, :]

    each_asked(me_ref, want_ref, packed, passed, use)
    products = dot_nt(stack[...], normed_own[...])
    masks = lane_masks(lens_ref, wanted, 0, normed_own.shape[0])
    out[...] = merged(products, masks, low).astype(bf16)


def attend(
    chunk, heads, kv_heads,
    index_ref, lens_ref, qkv, low0, low1, low2, low3, chosen, cosine, sine,
    q_gain, k_gain, out_w, old_k, old_v, after,
    new_k, new_v, *terms,
):
    rows = qkv.shape[0]
    width = out_w.shape[0]
    first = chunk * rows
    here = slice(first, first + rows)
    wanted, rank = chosen.shape[0], chosen.shape[1] // 3
    q_width, k_width = heads * HEAD_WIDTH, kv_heads * HEAD_WIDTH

    def stack(number, columns=slice(None)):
        block = chosen[:, number * rank : (number + 1) * rank, columns]
        return block.reshape(wanted * rank, block.shape[2])

    masks = lane_masks(lens_ref, wanted, first, rows)
    low = low0.shape[0]
    total = sum(ref[0:low, here].astype(f32) for ref in (low0, low1, low2, low3))
    total = total.astype(bf16).astype(f32)
    query = qkv[:, 0:q_width] + delta(total[0:rank], masks, stack(0))
    key = qkv[:, q_width : q_width + k_width] + delta(total[rank : 2 * rank], masks, stack(1, slice(0, k_width)))
    value = qkv[:, q_width + k_width :] + delta(total[2 * rank :], masks, stack(1, slice(k_width, 2 * k_width)))
    new_v[...] = value.astype(bf16)
    cos, sin = cosine[here, :], sine[here, :]

    def turn(values, gain):
        square = jnp.mean(values * values, axis=1, keepdims=True)
        values = values * lax.rsqrt(square + epsilon) * gain[...]
        return (values * cos + pltpu.roll(values, HEAD_WIDTH // 2, 1) * sin).astype(bf16)

    def head(h):
        return slice(h * HEAD_WIDTH, (h + 1) * HEAD_WIDTH)

    for h in range(kv_heads):
        new_k[:, head(h)] = turn(key[:, head(h)], k_gain)
    seen = first + rows
    starts, _ = bounds(lens_ref, wanted)
    down = lax.broadcasted_iota(jnp.int32, (rows, 1), 0) + first
    start_of = jnp.zeros((rows, 1), jnp.int32)
    for s in starts:
        start_of = jnp.where(down >= s, s, start_of)
    along = lax.broadcasted_iota(jnp.int32, (rows, seen), 1)
    allowed = (along <= down) & (along >= start_of)
    group = heads // kv_heads
    mixed = []
    for kv in range(kv_heads):
        keys, values = new_k[:, head(kv)], new_v[:, head(kv)]
        if chunk > 0:
            keys = jnp.concatenate([old_k[:, head(kv)], keys], axis=0)
            values = jnp.concatenate([old_v[:, head(kv)], values], axis=0)
        for h in range(kv * group, (kv + 1) * group):
            scores = dot_nt(turn(query[:, head(h)], q_gain), keys) * (1.0 / math.sqrt(HEAD_WIDTH))
            raw = jnp.where(allowed, jnp.exp(scores), 0.0)
            probs = (raw * (1.0 / jnp.sum(raw, axis=1, keepdims=True))).astype(bf16)
            mixed.append(dot(probs, values).astype(bf16))
    attended = jnp.concatenate(mixed, axis=1)
    lows = merged(dot_nt(stack(2), attended), masks, rank)
    share(index_ref, attended, out_w, lows, *terms)


def share(index_ref, values, weight, lows, keep, *sends):
    rows, width = values.shape[0], sends[0].shape[1]
    half = len(sends) // 2
    left, right = slice(0, width), slice(width, 2 * width)
    for rel, at in ((1, 0), (3, half)):
        term = dot(values, weight[:, part_of(index_ref, rel, width)]).astype(bf16)
        row = 0
        for target in sends[at : at + half]:
            count = min(target.shape[0], rows - row)
            target[0:count, :] = term[row : row + count, :]
            row += count
    sends[half - 1][-lows.shape[0] :, 0:rows] = lows.astype(bf16)
    for rel, at in ((0, left), (2, right)):
        keep[0:rows, at] = dot(values, weight[:, part_of(index_ref, rel, width)])
    keep[rows:, 0:rows] = lows


def add_pair(kept, *refs):
    *arrived, _, _, _, out = refs
    half = len(arrived) // 2
    width = out.shape[1] // 2
    for at, pieces in ((slice(0, width), arrived[:half]), (slice(width, 2 * width), arrived[half:])):
        row = 0
        for piece in pieces:
            here = slice(row, row + piece.shape[0])
            out[here, at] = (kept[here, at] + piece[...].astype(f32)).astype(bf16)
            row += piece.shape[0]


def residual(chunk, lens_ref, chip, arrived, own, across, table, table_across, after, *outs):
    half, width = outs[0].shape
    rows = 2 * half
    wanted = lens_ref.shape[1]
    rank = chip.shape[0] - rows
    low = table.shape[0] - wanted * rank
    left, right = slice(0, width), slice(width, 2 * width)
    masks = lane_masks(lens_ref, wanted, chunk * rows, rows)
    lows = chip[rows : rows + rank, 0:rows].astype(f32) + arrived[rows : rows + rank, 0:rows].astype(f32)
    lows = spread(lows.astype(bf16).astype(f32), masks)
    for number, (mine, theirs, tokens, b) in enumerate(
        ((left, right, own, table), (right, left, across, table_across))
    ):
        total = chip[0:rows, mine].astype(f32) + arrived[0:rows, theirs].astype(f32)
        total = total + dot_tn(lows, b[low:, :]).astype(bf16).astype(f32)
        total = (total + tokens[chunk * rows : (chunk + 1) * rows, :].astype(f32)).astype(bf16)
        outs[2 * number][...] = total[:half]
        outs[2 * number + 1][...] = total[half:]


def choose_second(first, count, sizes, me_ref, want_ref, *refs):
    packed, passed, outs = refs[:count], refs[count], refs[count + 2 :]
    unit = passed.shape[2]

    def use(slot, block):
        row = 0
        for number, start, height in sizes:
            out = outs[number]
            at = pl.ds(pl.multiple_of(start + slot * height, 16), height)
            for k in range(out.shape[1] // unit):
                out[at, k * unit : (k + 1) * unit] = block[row : row + height, :]
                row += height

    each_asked(me_ref, want_ref, packed, passed, use, first)


def feed_forward(
    chunk,
    index_ref, lens_ref, left0, left1, right0, right1, left2, left3, right2, right3,
    table0, table1, table2, table3, stack_a, stack_g, stack_u, gain, gate_w, up_w, down_w,
    *rest,
):
    *terms, normed, hidden = rest
    half, width = left0.shape
    rows = 2 * half
    wanted = lens_ref.shape[1]
    rank = stack_a.shape[0] // wanted
    low = table0.shape[0] // wanted - rank
    unit = math.gcd(width, hidden.shape[1])
    pieces = [pl.ds(k * unit, unit) for k in range(hidden.shape[1] // unit)]
    masks = lane_masks(lens_ref, wanted, chunk * rows, rows)
    for k, refs in enumerate(((left0, left2, right0, right2), (left1, left3, right1, right3))):
        loads = [lambda ref=ref: ref[...].astype(f32) for ref in refs]
        normalize(index_ref, loads, gain, normed.at[k * half : (k + 1) * half, :])
    products = sum(
        dot_nt(table[0 : wanted * low, :], normed[:, part_of(index_ref, rel, width)])
        for rel, table in enumerate((table0, table1, table2, table3))
    )
    total = merged(products, masks, low).astype(bf16).astype(f32)
    low_gate, low_up = spread(total[0:rank], masks), spread(total[rank:], masks)
    for piece in pieces:
        gate = dot(normed[...], gate_w[:, piece])
        gate = gate + dot_tn(low_gate, stack_g[:, piece]).astype(bf16).astype(f32)
        upward = dot(normed[...], up_w[:, piece])
        upward = upward + dot_tn(low_up, stack_u[:, piece]).astype(bf16).astype(f32)
        hidden[:, piece] = (gate / (1.0 + jnp.exp(-gate)) * upward).astype(bf16)
    lows = merged(dot_nt(stack_a[...], hidden[...]), masks, rank)
    share(index_ref, hidden[...], down_w, lows, *terms)


def split_pair(rank, kept, *refs):
    *arrived, _, stay, away = refs
    half = len(arrived) // 2
    width = away.shape[1]
    row = 0
    for piece in arrived[:half]:
        here = slice(row, row + piece.shape[0])
        stay[here, :] = kept[here, 0:width] + piece[...].astype(f32)
        row += piece.shape[0]
    row = 0
    for piece in arrived[half:]:
        here = slice(row, row + piece.shape[0])
        away[here, :] = (kept[here, width:] + piece[...].astype(f32)).astype(bf16)
        row += piece.shape[0]
    away[row:, :] = stay[row:, :].astype(bf16)


def finish(count, lens_ref, table, *refs):
    out = refs[-1]
    wanted = lens_ref.shape[1]
    width = out.shape[1]
    for c in range(count):
        stay, arrived, *resid = refs[4 * c : 4 * c + 4]
        half = resid[0].shape[0]
        rows = 2 * half
        masks = lane_masks(lens_ref, wanted, c * rows, rows)
        lows = stay[rows:, 0:rows] + arrived[rows:, 0:rows].astype(f32)
        total = stay[0:rows, :] + arrived[0:rows, :].astype(f32)
        total = total + delta(lows.astype(bf16).astype(f32), masks, table[...])
        for k, piece in enumerate(resid):
            at = slice(k * half, (k + 1) * half)
            out[c * rows + k * half : c * rows + (k + 1) * half, :] = (
                total[at, :] + piece[...].astype(f32)
            ).astype(bf16)


def rotation_tables(lens, row_count):
    half = HEAD_WIDTH // 2
    inverse = rope_base ** (-(jnp.arange(half, dtype=f32) * 2.0) / HEAD_WIDTH)
    row = jnp.arange(row_count, dtype=jnp.int32)
    start_of = jnp.zeros_like(row)
    start = jnp.int32(0)
    for j in range(lens.shape[0]):
        start_of = jnp.where(row >= start, start, start_of)
        start = start + lens[j]
    angle = (row - start_of).astype(f32)[:, None] * jnp.concatenate([inverse, inverse])[None, :]
    sign = jnp.concatenate([-jnp.ones(half, f32), jnp.ones(half, f32)])
    return jnp.cos(angle), jnp.sin(angle) * sign[None, :]


def swap_core(values):
    return lax.ppermute(values, "tp", [(k, k ^ 1) for k in range(4)])


def swap_across(values):
    return lax.ppermute(values, "tp", [(k, k ^ 2) for k in range(4)])


def swap_diagonal(values):
    return lax.ppermute(values, "tp", [(k, k ^ 3) for k in range(4)])


def swap_req(values, flips):
    return lax.ppermute(values, "req", [(k, k ^ flips) for k in range(lax.axis_size("req"))])


def per_device(
    tokens,
    lengths,
    request_adapter_index,
    attention_norm_gain,
    query_norm_gain,
    key_norm_gain,
    feedforward_norm_gain,
    query_weight,
    key_weight,
    value_weight,
    output_weight,
    gate_weight,
    up_weight,
    down_weight,
    query_key_value_adapter_input,
    output_adapter_input,
    gate_up_adapter_input,
    down_adapter_input,
    query_adapter_output,
    key_adapter_output,
    value_adapter_output,
    projection_adapter_output,
    gate_adapter_output,
    up_adapter_output,
    down_adapter_output,
):
    assert lax.axis_size("tp") == 4
    row_count, width = tokens.shape
    groups = lax.axis_size("req")
    wanted = lengths.shape[1]
    held, low_qkv, _ = query_key_value_adapter_input.shape
    rank = output_adapter_input.shape[1]
    low_gu = gate_up_adapter_input.shape[1]
    q_width, k_width = query_weight.shape[1], key_weight.shape[1]
    hidden_width = gate_weight.shape[1]
    heads, kv_heads = q_width // HEAD_WIDTH, k_width // HEAD_WIDTH
    unit = math.gcd(width, hidden_width)
    rows = row_count // CHUNKS
    assert width == q_width == 2 * k_width == row_count
    index = lax.axis_index("tp").astype(jnp.int32).reshape(1)
    me = lax.axis_index("req").astype(jnp.int32).reshape(1)
    want = request_adapter_index

    peers = groups // 2
    across = swap_across(tokens)
    core = swap_core(tokens)
    diagonal = swap_core(across)
    want_neighbour = swap_req(want, 1)

    def for_neighbour(blocks, after, heights):
        return call(
            functools.partial(pick_for_neighbour, len(blocks)),
            [SMEM] * 2 + [VMEM] * len(blocks) + [ANY],
            [shaped((peers, height, blocks[0].shape[2]), bf16) for height in heights],
        )(me, want_neighbour, *blocks, after)

    def loaded(weights, after, limit):
        return call(
            functools.partial(load, len(weights)), [ANY] * (len(weights) + len(after)),
            [shaped(w.shape, bf16) for w in weights],
            scratch=[pltpu.SemaphoreType.DMA((len(weights),))], limit=limit,
        )(*weights, *after)

    tables = (
        query_key_value_adapter_input, query_adapter_output, key_adapter_output, value_adapter_output,
        output_adapter_input, gate_up_adapter_input, projection_adapter_output, down_adapter_output,
        down_adapter_input, gate_adapter_output, up_adapter_output,
    )
    plan = (
        (0, (0, width), 0, 0),
        (1, (0, q_width), low_qkv, 0),
        (2, (0, k_width), low_qkv + rank, 0),
        (3, (0, k_width), low_qkv + rank, k_width),
        (4, (0, width), low_qkv + 2 * rank, 0),
    )
    plan_second, row = [], 0
    shapes = ((low_gu, width), (rank, width), (rank, width)) + ((rank, hidden_width),) * 3
    for table, (height, columns) in enumerate(shapes):
        for k in range(columns // unit):
            plan_second.append((5 + table, (k * unit, unit), row, 0))
            row += height
    block, block_second = call(
        functools.partial(gather_tables, (plan, tuple(plan_second))), [ANY] * len(tables),
        [shaped((held, low_qkv + 3 * rank, width), bf16), shaped((held, row, unit), bf16)],
        scratch=[pltpu.SemaphoreType.DMA((len(plan) + len(plan_second),))], limit=60,
    )(*tables)
    cosine, sine = rotation_tables(lengths[0], row_count)

    gain_one = attention_norm_gain.reshape(1, -1)
    gain_two = feedforward_norm_gain.reshape(1, -1)
    q_gain = query_norm_gain.reshape(1, -1)
    k_gain = key_norm_gain.reshape(1, -1)
    qkv_width = q_width + 2 * k_width
    normed_own, output_weight, *qkv = call(
        project_qkv, [SMEM] + [VMEM] * 5 + [HBM] * 4,
        [shaped((row_count, width), bf16), shaped(output_weight.shape, bf16)] + [shaped((rows, qkv_width), f32)] * CHUNKS,
        scratch=[
            pltpu.VMEM(query_weight.shape, bf16),
            pltpu.VMEM(key_weight.shape, bf16),
            pltpu.VMEM(value_weight.shape, bf16),
            pltpu.SemaphoreType.DMA((13,)),
        ],
        limit=50,
    )(
        index, tokens, core, across, diagonal, gain_one, query_weight, key_weight, value_weight,
        output_weight,
    )
    everyone = [block] + [swap_req(block, 2 * rel) for rel in range(1, peers)]
    (passing,) = for_neighbour(everyone, sine, [low_qkv + 3 * rank])
    block_second = call(hold, [VMEM, ANY], shaped(block_second.shape, bf16))(block_second, passing)
    second = [block_second] + [swap_req(block_second, 2 * rel) for rel in range(1, peers)]
    low, chosen = call(
        functools.partial(low_first, rank), [SMEM] * 3 + [VMEM] * (peers + 2) + [ANY] * 2,
        [
            shaped((low_qkv, row_count), bf16),
            shaped((wanted, 3 * rank, width), bf16),
        ],
        scratch=[pltpu.VMEM((wanted * low_qkv, width), bf16)],
    )(
        me, want, lengths, *everyone, swap_req(passing, 1), normed_own,
        cosine, sine,
    )
    lows = (low, swap_core(low), swap_across(low), swap_diagonal(low))

    tall = rows + rank
    cuts = [rows // 2, rows // 2 + rank, rows // 2, rows // 2]
    terms = [shaped((tall, 2 * width), f32)] + [shaped((cut, width), bf16) for cut in cuts]
    past = [jnp.zeros((16, k_width), bf16)] * 2
    after = low
    residuals = []
    for c in range(CHUNKS):
        new_k, new_v, keep, *sends = call(
            functools.partial(attend, c, heads, kv_heads),
            [SMEM] * 2 + [VMEM] * 13 + [ANY],
            [shaped((rows, k_width), bf16)] * 2 + terms,
        )(
            index, lengths, qkv[c], *lows, chosen, cosine, sine,
            q_gain, k_gain, output_weight, *past, after,
        )
        past = [new_k, new_v] if c == 0 else [
            jnp.concatenate([old, new], axis=0) for old, new in zip(past, (new_k, new_v))
        ]
        if c == 0:
            heights = [height * (columns // unit) for height, columns in shapes]
            cuts_second = [sum(heights[:2]), sum(heights[2:])]
            passing_second = for_neighbour(second, new_k, cuts_second)
        chip = call(add_pair, [VMEM] * 5 + [ANY] * 3, shaped((tall, 2 * width), bf16))(
            keep, *[swap_core(piece) for piece in sends], passing_second[0] if c == 0 else arrived,
            keep if c == 0 else table_across, keep if c == 0 else gate_weight,
        )
        after = chip
        if c == 0:
            def chosen_second(part, outs, sizes, after):
                return call(
                    functools.partial(choose_second, part * cuts_second[0], peers, sizes),
                    [SMEM] * 2 + [VMEM] * (peers + 1) + [ANY], outs,
                )(me, want, *second, swap_req(passing_second[part], 1), after)

            (table,) = chosen_second(
                0, [shaped((wanted * (low_gu + rank), width), bf16)],
                ((0, 0, low_gu), (0, wanted * low_gu, rank)), chip,
            )
            gate_weight, up_weight, down_weight = loaded(
                (gate_weight, up_weight, down_weight), (table,), 44
            )
            down_b, down_a, gate_b, up_b = chosen_second(
                1, [shaped((wanted * h, w), bf16) for h, w in shapes[2:]],
                tuple((k, 0, h) for k, (h, _) in enumerate(shapes[2:])), table,
            )
            table_across = swap_across(table)
            tables = (table, swap_core(table), table_across, swap_core(table_across))
        arrived = swap_across(chip)
        resid = call(
            functools.partial(residual, c), [SMEM] + [VMEM] * 6 + [ANY],
            [shaped((rows // 2, width), bf16)] * 4,
        )(
            lengths, chip, arrived, tokens, across, table, table_across, gate_weight,
        )
        residuals.append(resid)

    ends = []
    arrived = gate_weight
    for c in range(CHUNKS):
        resid = residuals[c]
        keep, *sends = call(
            functools.partial(feed_forward, c),
            [SMEM] * 2 + [VMEM] * 19,
            terms,
            limit=32,
            scratch=[
                pltpu.VMEM((rows, 4 * width), bf16),
                pltpu.VMEM((rows, hidden_width), bf16),
            ],
        )(
            index, lengths, *resid, *[swap_core(piece) for piece in resid], *tables, down_a, gate_b, up_b,
            gain_two, gate_weight, up_weight, down_weight,
        )
        stay, away = call(
            functools.partial(split_pair, rank), [VMEM] * 5 + [ANY],
            [shaped((tall, width), f32), shaped((tall, width), bf16)],
        )(keep, *[swap_core(piece) for piece in sends], arrived)
        after = away
        arrived = swap_across(away)
        ends += [stay, arrived, *resid[:2]]
    return call(
        functools.partial(finish, CHUNKS), [SMEM] + [VMEM] * (1 + 4 * CHUNKS),
        shaped((row_count, width), bf16),
    )(lengths, down_b, *ends)


def solution(mesh):
    placed = (
        P("req", "tp"),
        P("req", None),
        P("req", None),
        P(),
        P(),
        P(),
        P(),
        P(None, "tp"),
        P(None, "tp"),
        P(None, "tp"),
        P("tp", None),
        P(None, "tp"),
        P(None, "tp"),
        P("tp", None),
        P("req", None, "tp"),
        P("req", None, "tp"),
        P("req", None, "tp"),
        P("req", None, "tp"),
        P("req", None, "tp"),
        P("req", None, "tp"),
        P("req", None, "tp"),
        P("req", None, "tp"),
        P("req", None, "tp"),
        P("req", None, "tp"),
        P("req", None, "tp"),
    )
    return jax.shard_map(
        per_device, mesh=mesh, in_specs=placed, out_specs=P("req", "tp"), check_vma=False
    )
```

```python
import functools
import math

import jax
import jax.numpy as jnp
from jax import lax
from jax.experimental import pallas as pl
from jax.experimental.pallas import tpu as pltpu
from jax.sharding import PartitionSpec as P

HEAD_WIDTH = 128
CHUNKS = 2

epsilon = 1e-06
rope_base = 1000000.0

bf16 = jnp.bfloat16
f32 = jnp.float32
VMEM = pl.BlockSpec(memory_space=pltpu.VMEM)
ANY = pl.BlockSpec(memory_space=pl.ANY)
HBM = pl.BlockSpec(memory_space=pltpu.HBM)
SMEM = pl.BlockSpec(memory_space=pltpu.SMEM)


def call(body, in_specs, outs, scratch=(), limit=16, out_specs=None):
    single = not isinstance(outs, (list, tuple))
    if out_specs is None:
        out_specs = VMEM if single else [VMEM] * len(outs)
    return pl.pallas_call(
        body,
        out_shape=outs if single else list(outs),
        in_specs=in_specs,
        out_specs=out_specs,
        scratch_shapes=list(scratch),
        compiler_params=pltpu.CompilerParams(vmem_limit_bytes=limit * 1024 * 1024),
        cost_estimate=pl.CostEstimate(flops=1, bytes_accessed=1, transcendentals=0),
    )


def shaped(shape, dtype):
    return jax.ShapeDtypeStruct(shape, dtype)


def dot(a, b):
    return lax.dot_general(a, b, (((1,), (0,)), ((), ())), preferred_element_type=f32)


def dot_nt(a, b):
    return lax.dot_general(a, b, (((1,), (1,)), ((), ())), preferred_element_type=f32)


def dot_tn(a, b):
    return lax.dot_general(a, b, (((0,), (0,)), ((), ())), preferred_element_type=f32)


def part_of(index_ref, rel, width):
    return pl.ds(pl.multiple_of((index_ref[0] ^ rel) * width, width), width)


def bounds(lens_ref, count):
    starts, total = [], jnp.int32(0)
    for j in range(count):
        starts.append(total)
        total = total + lens_ref[0, j]
    return starts, starts[1:] + [total]


def lane_masks(lens_ref, count, first, width):
    starts, ends = bounds(lens_ref, count)
    rows = lax.broadcasted_iota(jnp.int32, (1, width), 1) + first
    return [((rows >= s) & (rows < e)).astype(f32) for s, e in zip(starts, ends)]


def spread(piece, masks):
    return jnp.concatenate([piece * m for m in masks], axis=0).astype(bf16)


def merged(products, masks, low):
    return sum(products[j * low : (j + 1) * low, :] * m for j, m in enumerate(masks))


def delta(piece, masks, stack):
    return dot_tn(spread(piece, masks), stack).astype(bf16).astype(f32)


def start_all(pairs, sems):
    copies = [pltpu.make_async_copy(a, b, sems.at[k]) for k, (a, b) in enumerate(pairs)]
    for copy in copies:
        copy.start()
    return copies


def gather_tables(plans, *refs):
    *refs, sems = refs
    pairs = []
    for plan, out in zip(plans, refs[-len(plans) :]):
        for table, columns, row, column in plan:
            source = refs[table]
            there = out.at[:, pl.ds(row, source.shape[1]), pl.ds(column, columns[1])]
            pairs.append((source.at[:, :, pl.ds(*columns)], there))
    for copy in start_all(pairs, sems):
        copy.wait()


def load(count, *refs):
    for copy in start_all(list(zip(refs[:count], refs[-1 - count : -1])), refs[-1]):
        copy.wait()


def owner_at(me_ref, rel, flip):
    return me_ref[0] ^ (2 * rel + flip)


def pick_for_neighbour(count, me_ref, want_ref, *refs):
    packed, sends = refs[:count], refs[count + 1 :]
    held = packed[0].shape[0]
    for rel, ref in enumerate(packed):
        owner = owner_at(me_ref, rel, 0)
        pick = jnp.int32(0)
        for j in range(want_ref.shape[1]):
            a = want_ref[0, j]
            pick = pick + jnp.where(a // held == owner, a % held, 0)
        row = 0
        for send in sends:
            height = send.shape[1]
            send[rel] = ref[pick, row : row + height, :]
            row += height


def hold(block, after, out):
    out[...] = block[...]


def each_asked(me_ref, want_ref, packed, passed, use, first=0):
    held = packed[0].shape[-3]
    for rel in range(passed.shape[0]):
        for flip in range(2):
            owner = owner_at(me_ref, rel, flip)
            slot, pick, found = jnp.int32(0), jnp.int32(0), jnp.int32(0)
            for j in range(want_ref.shape[1]):
                a = want_ref[0, j]
                hit = (a // held == owner).astype(jnp.int32)
                slot, pick, found = slot + hit * j, pick + hit * (a % held), found + hit

            @pl.when(found > 0)
            def _():
                rows = pl.ds(first, passed.shape[1])
                use(slot, passed.at[rel] if flip else packed[rel].at[pick, rows, :])


def normalize(index_ref, refs, gain, normed, keep_own=None):
    blocks = [load() for load in refs]
    width = blocks[0].shape[1]
    square = sum(jnp.sum(b * b, axis=1, keepdims=True) for b in blocks)
    scale = lax.rsqrt(square / (len(blocks) * width) + epsilon)
    for rel, block in enumerate(blocks):
        part = part_of(index_ref, rel, width)
        value = (block * scale * gain[:, part]).astype(bf16)
        normed[:, part] = value
        if rel == 0 and keep_own is not None:
            keep_own(value)


def project_qkv(
    index_ref, own, core, across, diagonal, gain, q_hbm, k_hbm, v_hbm, out_hbm,
    normed_own, out_w, *rest,
):
    *outs, q_w, k_w, v_w, sems = rest
    rows, width = own.shape[0] // len(outs), own.shape[1]
    q_width, k_width = q_w.shape[1], k_w.shape[1]
    parts = [part_of(index_ref, rel, width) for rel in range(4)]
    pairs = []
    for part in parts:
        pairs += [(a.at[part, :], b.at[part, :]) for a, b in ((q_hbm, q_w), (k_hbm, k_w), (v_hbm, v_w))]
    copies = start_all(pairs + [(out_hbm, out_w)], sems)
    scales = []
    for c in range(len(outs)):
        here = slice(c * rows, (c + 1) * rows)
        square = jnp.zeros((rows, 1), f32)
        for ref in (own, core, across, diagonal):
            block = ref[here, :].astype(f32)
            square = square + jnp.sum(block * block, axis=1, keepdims=True)
        scales.append(lax.rsqrt(square / (4 * width) + epsilon))
    for rel, ref in enumerate((own, core, across, diagonal)):
        part = parts[rel]
        for copy in copies[3 * rel : 3 * rel + 3]:
            copy.wait()
        for c, out in enumerate(outs):
            here = slice(c * rows, (c + 1) * rows)
            normed = (ref[here, :].astype(f32) * scales[c] * gain[:, part]).astype(bf16)
            if rel == 0:
                normed_own[here, :] = normed
            for w, low, high in (
                (q_w, 0, q_width),
                (k_w, q_width, q_width + k_width),
                (v_w, q_width + k_width, q_width + 2 * k_width),
            ):
                term = dot(normed, w[part, :])
                if rel == 0:
                    out[:, low:high] = term
                else:
                    out[:, low:high] += term
    copies[-1].wait()


def rows_of(slot, height):
    return pl.ds(pl.multiple_of(slot * height, 16), height)


def low_first(rank, me_ref, want_ref, lens_ref, *refs):
    *packed, passed, normed_own, _, _, out, chosen, stack = refs
    wanted = want_ref.shape[1]
    low = out.shape[0]

    def use(slot, block):
        stack[rows_of(slot, low), :] = block[0:low, :]
        chosen[slot] = block[low : low + 3 * rank, :]

    each_asked(me_ref, want_ref, packed, passed, use)
    products = dot_nt(stack[...], normed_own[...])
    masks = lane_masks(lens_ref, wanted, 0, normed_own.shape[0])
    out[...] = merged(products, masks, low).astype(bf16)


def attend(
    chunk, heads, kv_heads,
    index_ref, lens_ref, qkv, low0, low1, low2, low3, chosen, cosine, sine,
    q_gain, k_gain, out_w, old_k, old_v, after,
    new_k, new_v, *terms,
):
    rows = qkv.shape[0]
    width = out_w.shape[0]
    first = chunk * rows
    here = slice(first, first + rows)
    wanted, rank = chosen.shape[0], chosen.shape[1] // 3
    q_width, k_width = heads * HEAD_WIDTH, kv_heads * HEAD_WIDTH

    def stack(number, columns=slice(None)):
        block = chosen[:, number * rank : (number + 1) * rank, columns]
        return block.reshape(wanted * rank, block.shape[2])

    masks = lane_masks(lens_ref, wanted, first, rows)
    low = low0.shape[0]
    total = sum(ref[0:low, here].astype(f32) for ref in (low0, low1, low2, low3))
    total = total.astype(bf16).astype(f32)
    query = qkv[:, 0:q_width] + delta(total[0:rank], masks, stack(0))
    key = qkv[:, q_width : q_width + k_width] + delta(total[rank : 2 * rank], masks, stack(1, slice(0, k_width)))
    value = qkv[:, q_width + k_width :] + delta(total[2 * rank :], masks, stack(1, slice(k_width, 2 * k_width)))
    new_v[...] = value.astype(bf16)
    cos, sin = cosine[here, :], sine[here, :]

    def turn(values, gain):
        square = jnp.mean(values * values, axis=1, keepdims=True)
        values = values * lax.rsqrt(square + epsilon) * gain[...]
        return (values * cos + pltpu.roll(values, HEAD_WIDTH // 2, 1) * sin).astype(bf16)

    def head(h):
        return slice(h * HEAD_WIDTH, (h + 1) * HEAD_WIDTH)

    for h in range(kv_heads):
        new_k[:, head(h)] = turn(key[:, head(h)], k_gain)
    seen = first + rows
    starts, _ = bounds(lens_ref, wanted)
    down = lax.broadcasted_iota(jnp.int32, (rows, 1), 0) + first
    start_of = jnp.zeros((rows, 1), jnp.int32)
    for s in starts:
        start_of = jnp.where(down >= s, s, start_of)
    along = lax.broadcasted_iota(jnp.int32, (rows, seen), 1)
    allowed = (along <= down) & (along >= start_of)
    group = heads // kv_heads
    mixed = []
    for kv in range(kv_heads):
        keys, values = new_k[:, head(kv)], new_v[:, head(kv)]
        if chunk > 0:
            keys = jnp.concatenate([old_k[:, head(kv)], keys], axis=0)
            values = jnp.concatenate([old_v[:, head(kv)], values], axis=0)
        for h in range(kv * group, (kv + 1) * group):
            scores = dot_nt(turn(query[:, head(h)], q_gain), keys) * (1.0 / math.sqrt(HEAD_WIDTH))
            raw = jnp.where(allowed, jnp.exp(scores), 0.0)
            probs = (raw * (1.0 / jnp.sum(raw, axis=1, keepdims=True))).astype(bf16)
            mixed.append(dot(probs, values).astype(bf16))
    attended = jnp.concatenate(mixed, axis=1)
    lows = merged(dot_nt(stack(2), attended), masks, rank)
    share(index_ref, attended, out_w, lows, *terms)


def share(index_ref, values, weight, lows, keep, *sends):
    rows, width = values.shape[0], sends[0].shape[1]
    half = len(sends) // 2
    left, right = slice(0, width), slice(width, 2 * width)
    for rel, at in ((1, 0), (3, half)):
        term = dot(values, weight[:, part_of(index_ref, rel, width)]).astype(bf16)
        row = 0
        for target in sends[at : at + half]:
            count = min(target.shape[0], rows - row)
            target[0:count, :] = term[row : row + count, :]
            row += count
    sends[half - 1][-lows.shape[0] :, 0:rows] = lows.astype(bf16)
    for rel, at in ((0, left), (2, right)):
        keep[0:rows, at] = dot(values, weight[:, part_of(index_ref, rel, width)])
    keep[rows:, 0:rows] = lows


def add_pair(kept, *refs):
    *arrived, _, _, _, out = refs
    half = len(arrived) // 2
    width = out.shape[1] // 2
    for at, pieces in ((slice(0, width), arrived[:half]), (slice(width, 2 * width), arrived[half:])):
        row = 0
        for piece in pieces:
            here = slice(row, row + piece.shape[0])
            out[here, at] = (kept[here, at] + piece[...].astype(f32)).astype(bf16)
            row += piece.shape[0]


def residual(chunk, lens_ref, chip, arrived, own, across, table, table_across, after, *outs):
    half, width = outs[0].shape
    rows = 2 * half
    wanted = lens_ref.shape[1]
    rank = chip.shape[0] - rows
    low = table.shape[0] - wanted * rank
    left, right = slice(0, width), slice(width, 2 * width)
    masks = lane_masks(lens_ref, wanted, chunk * rows, rows)
    lows = chip[rows : rows + rank, 0:rows].astype(f32) + arrived[rows : rows + rank, 0:rows].astype(f32)
    lows = spread(lows.astype(bf16).astype(f32), masks)
    for number, (mine, theirs, tokens, b) in enumerate(
        ((left, right, own, table), (right, left, across, table_across))
    ):
        total = chip[0:rows, mine].astype(f32) + arrived[0:rows, theirs].astype(f32)
        total = total + dot_tn(lows, b[low:, :]).astype(bf16).astype(f32)
        total = (total + tokens[chunk * rows : (chunk + 1) * rows, :].astype(f32)).astype(bf16)
        outs[2 * number][...] = total[:half]
        outs[2 * number + 1][...] = total[half:]


def choose_second(first, count, sizes, me_ref, want_ref, *refs):
    packed, passed, outs = refs[:count], refs[count], refs[count + 2 :]
    unit = passed.shape[2]

    def use(slot, block):
        row = 0
        for number, start, height in sizes:
            out = outs[number]
            at = pl.ds(pl.multiple_of(start + slot * height, 16), height)
            for k in range(out.shape[1] // unit):
                out[at, k * unit : (k + 1) * unit] = block[row : row + height, :]
                row += height

    each_asked(me_ref, want_ref, packed, passed, use, first)


def feed_forward(
    chunk,
    index_ref, lens_ref, left0, left1, right0, right1, left2, left3, right2, right3,
    table0, table1, table2, table3, stack_a, stack_g, stack_u, gain, gate_w, up_w, down_w,
    *rest,
):
    *terms, normed, hidden = rest
    half, width = left0.shape
    rows = 2 * half
    wanted = lens_ref.shape[1]
    rank = stack_a.shape[0] // wanted
    low = table0.shape[0] // wanted - rank
    unit = math.gcd(width, hidden.shape[1])
    pieces = [pl.ds(k * unit, unit) for k in range(hidden.shape[1] // unit)]
    masks = lane_masks(lens_ref, wanted, chunk * rows, rows)
    for k, refs in enumerate(((left0, left2, right0, right2), (left1, left3, right1, right3))):
        loads = [lambda ref=ref: ref[...].astype(f32) for ref in refs]
        normalize(index_ref, loads, gain, normed.at[k * half : (k + 1) * half, :])
    products = sum(
        dot_nt(table[0 : wanted * low, :], normed[:, part_of(index_ref, rel, width)])
        for rel, table in enumerate((table0, table1, table2, table3))
    )
    total = merged(products, masks, low).astype(bf16).astype(f32)
    low_gate, low_up = spread(total[0:rank], masks), spread(total[rank:], masks)
    for piece in pieces:
        gate = dot(normed[...], gate_w[:, piece])
        gate = gate + dot_tn(low_gate, stack_g[:, piece]).astype(bf16).astype(f32)
        upward = dot(normed[...], up_w[:, piece])
        upward = upward + dot_tn(low_up, stack_u[:, piece]).astype(bf16).astype(f32)
        hidden[:, piece] = (gate / (1.0 + jnp.exp(-gate)) * upward).astype(bf16)
    lows = merged(dot_nt(stack_a[...], hidden[...]), masks, rank)
    share(index_ref, hidden[...], down_w, lows, *terms)


def split_pair(rank, kept, *refs):
    *arrived, _, stay, away = refs
    half = len(arrived) // 2
    width = away.shape[1]
    row = 0
    for piece in arrived[:half]:
        here = slice(row, row + piece.shape[0])
        stay[here, :] = kept[here, 0:width] + piece[...].astype(f32)
        row += piece.shape[0]
    row = 0
    for piece in arrived[half:]:
        here = slice(row, row + piece.shape[0])
        away[here, :] = (kept[here, width:] + piece[...].astype(f32)).astype(bf16)
        row += piece.shape[0]
    away[row:, :] = stay[row:, :].astype(bf16)


def finish(count, lens_ref, table, *refs):
    out = refs[-1]
    wanted = lens_ref.shape[1]
    width = out.shape[1]
    for c in range(count):
        stay, arrived, *resid = refs[4 * c : 4 * c + 4]
        half = resid[0].shape[0]
        rows = 2 * half
        masks = lane_masks(lens_ref, wanted, c * rows, rows)
        lows = stay[rows:, 0:rows] + arrived[rows:, 0:rows].astype(f32)
        total = stay[0:rows, :] + arrived[0:rows, :].astype(f32)
        total = total + delta(lows.astype(bf16).astype(f32), masks, table[...])
        for k, piece in enumerate(resid):
            at = slice(k * half, (k + 1) * half)
            out[c * rows + k * half : c * rows + (k + 1) * half, :] = (
                total[at, :] + piece[...].astype(f32)
            ).astype(bf16)


def rotation_tables(lens, row_count):
    half = HEAD_WIDTH // 2
    inverse = rope_base ** (-(jnp.arange(half, dtype=f32) * 2.0) / HEAD_WIDTH)
    row = jnp.arange(row_count, dtype=jnp.int32)
    start_of = jnp.zeros_like(row)
    start = jnp.int32(0)
    for j in range(lens.shape[0]):
        start_of = jnp.where(row >= start, start, start_of)
        start = start + lens[j]
    angle = (row - start_of).astype(f32)[:, None] * jnp.concatenate([inverse, inverse])[None, :]
    sign = jnp.concatenate([-jnp.ones(half, f32), jnp.ones(half, f32)])
    return jnp.cos(angle), jnp.sin(angle) * sign[None, :]


def swap_core(values):
    return lax.ppermute(values, "tp", [(k, k ^ 1) for k in range(4)])


def swap_across(values):
    return lax.ppermute(values, "tp", [(k, k ^ 2) for k in range(4)])


def swap_diagonal(values):
    return lax.ppermute(values, "tp", [(k, k ^ 3) for k in range(4)])


def swap_req(values, flips):
    return lax.ppermute(values, "req", [(k, k ^ flips) for k in range(lax.axis_size("req"))])


def per_device(
    tokens,
    lengths,
    request_adapter_index,
    attention_norm_gain,
    query_norm_gain,
    key_norm_gain,
    feedforward_norm_gain,
    query_weight,
    key_weight,
    value_weight,
    output_weight,
    gate_weight,
    up_weight,
    down_weight,
    query_key_value_adapter_input,
    output_adapter_input,
    gate_up_adapter_input,
    down_adapter_input,
    query_adapter_output,
    key_adapter_output,
    value_adapter_output,
    projection_adapter_output,
    gate_adapter_output,
    up_adapter_output,
    down_adapter_output,
):
    assert lax.axis_size("tp") == 4
    row_count, width = tokens.shape
    groups = lax.axis_size("req")
    wanted = lengths.shape[1]
    held, low_qkv, _ = query_key_value_adapter_input.shape
    rank = output_adapter_input.shape[1]
    low_gu = gate_up_adapter_input.shape[1]
    q_width, k_width = query_weight.shape[1], key_weight.shape[1]
    hidden_width = gate_weight.shape[1]
    heads, kv_heads = q_width // HEAD_WIDTH, k_width // HEAD_WIDTH
    unit = math.gcd(width, hidden_width)
    rows = row_count // CHUNKS
    assert width == q_width == 2 * k_width == row_count
    index = lax.axis_index("tp").astype(jnp.int32).reshape(1)
    me = lax.axis_index("req").astype(jnp.int32).reshape(1)
    want = request_adapter_index

    peers = groups // 2
    across = swap_across(tokens)
    core = swap_core(tokens)
    diagonal = swap_core(across)
    want_neighbour = swap_req(want, 1)

    def for_neighbour(blocks, after, heights):
        return call(
            functools.partial(pick_for_neighbour, len(blocks)),
            [SMEM] * 2 + [VMEM] * len(blocks) + [ANY],
            [shaped((peers, height, blocks[0].shape[2]), bf16) for height in heights],
        )(me, want_neighbour, *blocks, after)

    def loaded(weights, after, limit):
        return call(
            functools.partial(load, len(weights)), [ANY] * (len(weights) + len(after)),
            [shaped(w.shape, bf16) for w in weights],
            scratch=[pltpu.SemaphoreType.DMA((len(weights),))], limit=limit,
        )(*weights, *after)

    tables = (
        query_key_value_adapter_input, query_adapter_output, key_adapter_output, value_adapter_output,
        output_adapter_input, gate_up_adapter_input, projection_adapter_output, down_adapter_output,
        down_adapter_input, gate_adapter_output, up_adapter_output,
    )
    plan = (
        (0, (0, width), 0, 0),
        (1, (0, q_width), low_qkv, 0),
        (2, (0, k_width), low_qkv + rank, 0),
        (3, (0, k_width), low_qkv + rank, k_width),
        (4, (0, width), low_qkv + 2 * rank, 0),
    )
    plan_second, row = [], 0
    shapes = ((low_gu, width), (rank, width), (rank, width)) + ((rank, hidden_width),) * 3
    for table, (height, columns) in enumerate(shapes):
        for k in range(columns // unit):
            plan_second.append((5 + table, (k * unit, unit), row, 0))
            row += height
    block, block_second = call(
        functools.partial(gather_tables, (plan, tuple(plan_second))), [ANY] * len(tables),
        [shaped((held, low_qkv + 3 * rank, width), bf16), shaped((held, row, unit), bf16)],
        scratch=[pltpu.SemaphoreType.DMA((len(plan) + len(plan_second),))], limit=60,
    )(*tables)
    cosine, sine = rotation_tables(lengths[0], row_count)

    gain_one = attention_norm_gain.reshape(1, -1)
    gain_two = feedforward_norm_gain.reshape(1, -1)
    q_gain = query_norm_gain.reshape(1, -1)
    k_gain = key_norm_gain.reshape(1, -1)
    qkv_width = q_width + 2 * k_width
    normed_own, output_weight, *qkv = call(
        project_qkv, [SMEM] + [VMEM] * 5 + [HBM] * 4,
        [shaped((row_count, width), bf16), shaped(output_weight.shape, bf16)] + [shaped((rows, qkv_width), f32)] * CHUNKS,
        scratch=[
            pltpu.VMEM(query_weight.shape, bf16),
            pltpu.VMEM(key_weight.shape, bf16),
            pltpu.VMEM(value_weight.shape, bf16),
            pltpu.SemaphoreType.DMA((13,)),
        ],
        limit=49,
    )(
        index, tokens, core, across, diagonal, gain_one, query_weight, key_weight, value_weight,
        output_weight,
    )
    everyone = [block] + [swap_req(block, 2 * rel) for rel in range(1, peers)]
    everyone[0] = call(hold, [VMEM, ANY], shaped(block.shape, bf16))(block, sine)
    (passing,) = for_neighbour(everyone, sine, [low_qkv + 3 * rank])
    block_second = call(hold, [VMEM, ANY], shaped(block_second.shape, bf16))(block_second, passing)
    second = [block_second] + [swap_req(block_second, 2 * rel) for rel in range(1, peers)]
    low, chosen = call(
        functools.partial(low_first, rank), [SMEM] * 3 + [VMEM] * (peers + 2) + [ANY] * 2,
        [
            shaped((low_qkv, row_count), bf16),
            shaped((wanted, 3 * rank, width), bf16),
        ],
        scratch=[pltpu.VMEM((wanted * low_qkv, width), bf16)],
    )(
        me, want, lengths, *everyone, swap_req(passing, 1), normed_own,
        cosine, sine,
    )
    lows = (low, swap_core(low), swap_across(low), swap_diagonal(low))

    tall = rows + rank
    cuts = [rows // 2, rows // 2 + rank, rows // 2, rows // 2]
    terms = [shaped((tall, 2 * width), f32)] + [shaped((cut, width), bf16) for cut in cuts]
    past = [jnp.zeros((16, k_width), bf16)] * 2
    after = low
    residuals = []
    for c in range(CHUNKS):
        new_k, new_v, keep, *sends = call(
            functools.partial(attend, c, heads, kv_heads),
            [SMEM] * 2 + [VMEM] * 13 + [ANY],
            [shaped((rows, k_width), bf16)] * 2 + terms,
        )(
            index, lengths, qkv[c], *lows, chosen, cosine, sine,
            q_gain, k_gain, output_weight, *past, after,
        )
        past = [new_k, new_v] if c == 0 else [
            jnp.concatenate([old, new], axis=0) for old, new in zip(past, (new_k, new_v))
        ]
        if c == 0:
            heights = [height * (columns // unit) for height, columns in shapes]
            cuts_second = [sum(heights[:2]), sum(heights[2:])]
            passing_second = for_neighbour(second, new_k, cuts_second)
        chip = call(add_pair, [VMEM] * 5 + [ANY] * 3, shaped((tall, 2 * width), bf16))(
            keep, *[swap_core(piece) for piece in sends], passing_second[0] if c == 0 else arrived,
            keep if c == 0 else table_across, keep if c == 0 else gate_weight,
        )
        after = chip
        if c == 0:
            def chosen_second(part, outs, sizes, after):
                return call(
                    functools.partial(choose_second, part * cuts_second[0], peers, sizes),
                    [SMEM] * 2 + [VMEM] * (peers + 1) + [ANY], outs,
                )(me, want, *second, swap_req(passing_second[part], 1), after)

            (table,) = chosen_second(
                0, [shaped((wanted * (low_gu + rank), width), bf16)],
                ((0, 0, low_gu), (0, wanted * low_gu, rank)), chip,
            )
            gate_weight, up_weight, down_weight = loaded(
                (gate_weight, up_weight, down_weight), (table,), 44
            )
            down_b, down_a, gate_b, up_b = chosen_second(
                1, [shaped((wanted * h, w), bf16) for h, w in shapes[2:]],
                tuple((k, 0, h) for k, (h, _) in enumerate(shapes[2:])), table,
            )
            table_across = swap_across(table)
            tables = (table, swap_core(table), table_across, swap_core(table_across))
        arrived = swap_across(chip)
        resid = call(
            functools.partial(residual, c), [SMEM] + [VMEM] * 6 + [ANY],
            [shaped((rows // 2, width), bf16)] * 4,
        )(
            lengths, chip, arrived, tokens, across, table, table_across, gate_weight,
        )
        residuals.append(resid)

    ends = []
    arrived = gate_weight
    for c in range(CHUNKS):
        resid = residuals[c]
        keep, *sends = call(
            functools.partial(feed_forward, c),
            [SMEM] * 2 + [VMEM] * 19,
            terms,
            limit=32,
            scratch=[
                pltpu.VMEM((rows, 4 * width), bf16),
                pltpu.VMEM((rows, hidden_width), bf16),
            ],
        )(
            index, lengths, *resid, *[swap_core(piece) for piece in resid], *tables, down_a, gate_b, up_b,
            gain_two, gate_weight, up_weight, down_weight,
        )
        stay, away = call(
            functools.partial(split_pair, rank), [VMEM] * 5 + [ANY],
            [shaped((tall, width), f32), shaped((tall, width), bf16)],
        )(keep, *[swap_core(piece) for piece in sends], arrived)
        after = away
        arrived = swap_across(away)
        ends += [stay, arrived, *resid[:2]]
    return call(
        functools.partial(finish, CHUNKS), [SMEM] + [VMEM] * (1 + 4 * CHUNKS),
        shaped((row_count, width), bf16),
    )(lengths, down_b, *ends)


def solution(mesh):
    placed = (
        P("req", "tp"),
        P("req", None),
        P("req", None),
        P(),
        P(),
        P(),
        P(),
        P(None, "tp"),
        P(None, "tp"),
        P(None, "tp"),
        P("tp", None),
        P(None, "tp"),
        P(None, "tp"),
        P("tp", None),
        P("req", None, "tp"),
        P("req", None, "tp"),
        P("req", None, "tp"),
        P("req", None, "tp"),
        P("req", None, "tp"),
        P("req", None, "tp"),
        P("req", None, "tp"),
        P("req", None, "tp"),
        P("req", None, "tp"),
        P("req", None, "tp"),
        P("req", None, "tp"),
    )
    return jax.shard_map(
        per_device, mesh=mesh, in_specs=placed, out_specs=P("req", "tp"), check_vma=False
    )
```

```python
import functools
import math

import jax
import jax.numpy as jnp
from jax import lax
from jax.experimental import pallas as pl
from jax.experimental.pallas import tpu as pltpu
from jax.sharding import PartitionSpec as P

HEAD_WIDTH = 128
CHUNKS = 2

epsilon = 1e-06
rope_base = 1000000.0

bf16 = jnp.bfloat16
f32 = jnp.float32
VMEM = pl.BlockSpec(memory_space=pltpu.VMEM)
ANY = pl.BlockSpec(memory_space=pl.ANY)
HBM = pl.BlockSpec(memory_space=pltpu.HBM)
SMEM = pl.BlockSpec(memory_space=pltpu.SMEM)


def call(body, in_specs, outs, scratch=(), limit=16, out_specs=None):
    single = not isinstance(outs, (list, tuple))
    if out_specs is None:
        out_specs = VMEM if single else [VMEM] * len(outs)
    return pl.pallas_call(
        body,
        out_shape=outs if single else list(outs),
        in_specs=in_specs,
        out_specs=out_specs,
        scratch_shapes=list(scratch),
        compiler_params=pltpu.CompilerParams(vmem_limit_bytes=limit * 1024 * 1024),
        cost_estimate=pl.CostEstimate(flops=1, bytes_accessed=1, transcendentals=0),
    )


def shaped(shape, dtype):
    return jax.ShapeDtypeStruct(shape, dtype)


def dot(a, b):
    return lax.dot_general(a, b, (((1,), (0,)), ((), ())), preferred_element_type=f32)


def dot_nt(a, b):
    return lax.dot_general(a, b, (((1,), (1,)), ((), ())), preferred_element_type=f32)


def dot_tn(a, b):
    return lax.dot_general(a, b, (((0,), (0,)), ((), ())), preferred_element_type=f32)


def part_of(index_ref, rel, width):
    return pl.ds(pl.multiple_of((index_ref[0] ^ rel) * width, width), width)


def bounds(lens_ref, count):
    starts, total = [], jnp.int32(0)
    for j in range(count):
        starts.append(total)
        total = total + lens_ref[0, j]
    return starts, starts[1:] + [total]


def lane_masks(lens_ref, count, first, width):
    starts, ends = bounds(lens_ref, count)
    rows = lax.broadcasted_iota(jnp.int32, (1, width), 1) + first
    return [((rows >= s) & (rows < e)).astype(f32) for s, e in zip(starts, ends)]


def spread(piece, masks):
    return jnp.concatenate([piece * m for m in masks], axis=0).astype(bf16)


def merged(products, masks, low):
    return sum(products[j * low : (j + 1) * low, :] * m for j, m in enumerate(masks))


def delta(piece, masks, stack):
    return dot_tn(spread(piece, masks), stack).astype(bf16).astype(f32)


def start_all(pairs, sems):
    copies = [pltpu.make_async_copy(a, b, sems.at[k]) for k, (a, b) in enumerate(pairs)]
    for copy in copies:
        copy.start()
    return copies


def gather_tables(plans, *refs):
    *refs, sems = refs
    pairs = []
    for plan, out in zip(plans, refs[-len(plans) :]):
        for table, columns, row, column in plan:
            source = refs[table]
            there = out.at[:, pl.ds(row, source.shape[1]), pl.ds(column, columns[1])]
            pairs.append((source.at[:, :, pl.ds(*columns)], there))
    for copy in start_all(pairs, sems):
        copy.wait()


def load(count, *refs):
    for copy in start_all(list(zip(refs[:count], refs[-1 - count : -1])), refs[-1]):
        copy.wait()


def owner_at(me_ref, rel, flip):
    return me_ref[0] ^ (2 * rel + flip)


def pick_for_neighbour(count, me_ref, want_ref, *refs):
    packed, sends = refs[:count], refs[count + 1 :]
    held = packed[0].shape[0]
    for rel, ref in enumerate(packed):
        owner = owner_at(me_ref, rel, 0)
        pick = jnp.int32(0)
        for j in range(want_ref.shape[1]):
            a = want_ref[0, j]
            pick = pick + jnp.where(a // held == owner, a % held, 0)
        row = 0
        for send in sends:
            height = send.shape[1]
            send[rel] = ref[pick, row : row + height, :]
            row += height


def hold(block, after, out):
    out[...] = block[...]


def each_asked(me_ref, want_ref, packed, passed, use, first=0):
    held = packed[0].shape[-3]
    for rel in range(passed.shape[0]):
        for flip in range(2):
            owner = owner_at(me_ref, rel, flip)
            slot, pick, found = jnp.int32(0), jnp.int32(0), jnp.int32(0)
            for j in range(want_ref.shape[1]):
                a = want_ref[0, j]
                hit = (a // held == owner).astype(jnp.int32)
                slot, pick, found = slot + hit * j, pick + hit * (a % held), found + hit

            @pl.when(found > 0)
            def _():
                rows = pl.ds(first, passed.shape[1])
                use(slot, passed.at[rel] if flip else packed[rel].at[pick, rows, :])


def normalize(index_ref, refs, gain, normed, keep_own=None):
    blocks = [load() for load in refs]
    width = blocks[0].shape[1]
    square = sum(jnp.sum(b * b, axis=1, keepdims=True) for b in blocks)
    scale = lax.rsqrt(square / (len(blocks) * width) + epsilon)
    for rel, block in enumerate(blocks):
        part = part_of(index_ref, rel, width)
        value = (block * scale * gain[:, part]).astype(bf16)
        normed[:, part] = value
        if rel == 0 and keep_own is not None:
            keep_own(value)


def project_qkv(
    index_ref, own, core, across, diagonal, gain, q_hbm, k_hbm, v_hbm, out_hbm,
    normed_own, out_w, *rest,
):
    *outs, q_w, k_w, v_w, sems = rest
    rows, width = own.shape[0] // len(outs), own.shape[1]
    q_width, k_width = q_w.shape[1], k_w.shape[1]
    parts = [part_of(index_ref, rel, width) for rel in range(4)]
    pairs = []
    for part in parts:
        pairs += [(a.at[part, :], b.at[part, :]) for a, b in ((q_hbm, q_w), (k_hbm, k_w), (v_hbm, v_w))]
    copies = start_all(pairs + [(out_hbm, out_w)], sems)
    scales = []
    for c in range(len(outs)):
        here = slice(c * rows, (c + 1) * rows)
        square = jnp.zeros((rows, 1), f32)
        for ref in (own, core, across, diagonal):
            block = ref[here, :].astype(f32)
            square = square + jnp.sum(block * block, axis=1, keepdims=True)
        scales.append(lax.rsqrt(square / (4 * width) + epsilon))
    for rel, ref in enumerate((own, core, across, diagonal)):
        part = parts[rel]
        for copy in copies[3 * rel : 3 * rel + 3]:
            copy.wait()
        for c, out in enumerate(outs):
            here = slice(c * rows, (c + 1) * rows)
            normed = (ref[here, :].astype(f32) * scales[c] * gain[:, part]).astype(bf16)
            if rel == 0:
                normed_own[here, :] = normed
            for w, low, high in (
                (q_w, 0, q_width),
                (k_w, q_width, q_width + k_width),
                (v_w, q_width + k_width, q_width + 2 * k_width),
            ):
                term = dot(normed, w[part, :])
                if rel == 0:
                    out[:, low:high] = term
                else:
                    out[:, low:high] += term
    copies[-1].wait()


def rows_of(slot, height):
    return pl.ds(pl.multiple_of(slot * height, 16), height)


def low_first(rank, me_ref, want_ref, lens_ref, *refs):
    *packed, passed, normed_own, _, _, out, chosen, stack = refs
    wanted = want_ref.shape[1]
    low = out.shape[0]

    def use(slot, block):
        stack[rows_of(slot, low), :] = block[0:low, :]
        chosen[slot] = block[low : low + 3 * rank, :]

    each_asked(me_ref, want_ref, packed, passed, use)
    products = dot_nt(stack[...], normed_own[...])
    masks = lane_masks(lens_ref, wanted, 0, normed_own.shape[0])
    out[...] = merged(products, masks, low).astype(bf16)


def attend(
    chunk, heads, kv_heads,
    index_ref, lens_ref, qkv, low0, low1, low2, low3, chosen, cosine, sine,
    q_gain, k_gain, out_w, old_k, old_v, after,
    new_k, new_v, *terms,
):
    rows = qkv.shape[0]
    width = out_w.shape[0]
    first = chunk * rows
    here = slice(first, first + rows)
    wanted, rank = chosen.shape[0], chosen.shape[1] // 3
    q_width, k_width = heads * HEAD_WIDTH, kv_heads * HEAD_WIDTH

    def stack(number, columns=slice(None)):
        block = chosen[:, number * rank : (number + 1) * rank, columns]
        return block.reshape(wanted * rank, block.shape[2])

    masks = lane_masks(lens_ref, wanted, first, rows)
    low = low0.shape[0]
    total = sum(ref[0:low, here].astype(f32) for ref in (low0, low1, low2, low3))
    total = total.astype(bf16).astype(f32)
    query = qkv[:, 0:q_width] + delta(total[0:rank], masks, stack(0))
    key = qkv[:, q_width : q_width + k_width] + delta(total[rank : 2 * rank], masks, stack(1, slice(0, k_width)))
    value = qkv[:, q_width + k_width :] + delta(total[2 * rank :], masks, stack(1, slice(k_width, 2 * k_width)))
    new_v[...] = value.astype(bf16)
    cos, sin = cosine[here, :], sine[here, :]

    def turn(values, gain):
        square = jnp.mean(values * values, axis=1, keepdims=True)
        values = values * lax.rsqrt(square + epsilon) * gain[...]
        return (values * cos + pltpu.roll(values, HEAD_WIDTH // 2, 1) * sin).astype(bf16)

    def head(h):
        return slice(h * HEAD_WIDTH, (h + 1) * HEAD_WIDTH)

    for h in range(kv_heads):
        new_k[:, head(h)] = turn(key[:, head(h)], k_gain)
    seen = first + rows
    starts, _ = bounds(lens_ref, wanted)
    down = lax.broadcasted_iota(jnp.int32, (rows, 1), 0) + first
    start_of = jnp.zeros((rows, 1), jnp.int32)
    for s in starts:
        start_of = jnp.where(down >= s, s, start_of)
    along = lax.broadcasted_iota(jnp.int32, (rows, seen), 1)
    allowed = (along <= down) & (along >= start_of)
    group = heads // kv_heads
    mixed = []
    for kv in range(kv_heads):
        keys, values = new_k[:, head(kv)], new_v[:, head(kv)]
        if chunk > 0:
            keys = jnp.concatenate([old_k[:, head(kv)], keys], axis=0)
            values = jnp.concatenate([old_v[:, head(kv)], values], axis=0)
        for h in range(kv * group, (kv + 1) * group):
            scores = dot_nt(turn(query[:, head(h)], q_gain), keys) * (1.0 / math.sqrt(HEAD_WIDTH))
            raw = jnp.where(allowed, jnp.exp(scores), 0.0)
            probs = (raw * (1.0 / jnp.sum(raw, axis=1, keepdims=True))).astype(bf16)
            mixed.append(dot(probs, values).astype(bf16))
    attended = jnp.concatenate(mixed, axis=1)
    lows = merged(dot_nt(stack(2), attended), masks, rank)
    share(index_ref, attended, out_w, lows, *terms)


def share(index_ref, values, weight, lows, keep, *sends):
    rows, width = values.shape[0], sends[0].shape[1]
    half = len(sends) // 2
    left, right = slice(0, width), slice(width, 2 * width)
    for rel, at in ((1, 0), (3, half)):
        term = dot(values, weight[:, part_of(index_ref, rel, width)]).astype(bf16)
        row = 0
        for target in sends[at : at + half]:
            count = min(target.shape[0], rows - row)
            target[0:count, :] = term[row : row + count, :]
            row += count
    sends[half - 1][-lows.shape[0] :, 0:rows] = lows.astype(bf16)
    for rel, at in ((0, left), (2, right)):
        keep[0:rows, at] = dot(values, weight[:, part_of(index_ref, rel, width)])
    keep[rows:, 0:rows] = lows


def add_pair(kept, *refs):
    *arrived, _, _, _, out = refs
    half = len(arrived) // 2
    width = out.shape[1] // 2
    for at, pieces in ((slice(0, width), arrived[:half]), (slice(width, 2 * width), arrived[half:])):
        row = 0
        for piece in pieces:
            here = slice(row, row + piece.shape[0])
            out[here, at] = (kept[here, at] + piece[...].astype(f32)).astype(bf16)
            row += piece.shape[0]


def residual(chunk, lens_ref, chip, arrived, own, across, table, table_across, after, *outs):
    half, width = outs[0].shape
    rows = 2 * half
    wanted = lens_ref.shape[1]
    rank = chip.shape[0] - rows
    low = table.shape[0] - wanted * rank
    left, right = slice(0, width), slice(width, 2 * width)
    masks = lane_masks(lens_ref, wanted, chunk * rows, rows)
    lows = chip[rows : rows + rank, 0:rows].astype(f32) + arrived[rows : rows + rank, 0:rows].astype(f32)
    lows = spread(lows.astype(bf16).astype(f32), masks)
    for number, (mine, theirs, tokens, b) in enumerate(
        ((left, right, own, table), (right, left, across, table_across))
    ):
        total = chip[0:rows, mine].astype(f32) + arrived[0:rows, theirs].astype(f32)
        total = total + dot_tn(lows, b[low:, :]).astype(bf16).astype(f32)
        total = (total + tokens[chunk * rows : (chunk + 1) * rows, :].astype(f32)).astype(bf16)
        outs[2 * number][...] = total[:half]
        outs[2 * number + 1][...] = total[half:]


def choose_second(first, count, sizes, me_ref, want_ref, *refs):
    packed, passed, outs = refs[:count], refs[count], refs[count + 2 :]
    unit = passed.shape[2]

    def use(slot, block):
        row = 0
        for number, start, height in sizes:
            out = outs[number]
            at = pl.ds(pl.multiple_of(start + slot * height, 16), height)
            for k in range(out.shape[1] // unit):
                out[at, k * unit : (k + 1) * unit] = block[row : row + height, :]
                row += height

    each_asked(me_ref, want_ref, packed, passed, use, first)


def feed_forward(
    chunk,
    index_ref, lens_ref, left0, left1, right0, right1, left2, left3, right2, right3,
    table0, table1, table2, table3, stack_a, stack_g, stack_u, gain, gate_w, up_w, down_w,
    *rest,
):
    *terms, normed, hidden = rest
    half, width = left0.shape
    rows = 2 * half
    wanted = lens_ref.shape[1]
    rank = stack_a.shape[0] // wanted
    low = table0.shape[0] // wanted - rank
    unit = math.gcd(width, hidden.shape[1])
    pieces = [pl.ds(k * unit, unit) for k in range(hidden.shape[1] // unit)]
    masks = lane_masks(lens_ref, wanted, chunk * rows, rows)
    for k, refs in enumerate(((left0, left2, right0, right2), (left1, left3, right1, right3))):
        loads = [lambda ref=ref: ref[...].astype(f32) for ref in refs]
        normalize(index_ref, loads, gain, normed.at[k * half : (k + 1) * half, :])
    products = sum(
        dot_nt(table[0 : wanted * low, :], normed[:, part_of(index_ref, rel, width)])
        for rel, table in enumerate((table0, table1, table2, table3))
    )
    total = merged(products, masks, low).astype(bf16).astype(f32)
    low_gate, low_up = spread(total[0:rank], masks), spread(total[rank:], masks)
    for piece in pieces:
        gate = dot(normed[...], gate_w[:, piece])
        gate = gate + dot_tn(low_gate, stack_g[:, piece]).astype(bf16).astype(f32)
        upward = dot(normed[...], up_w[:, piece])
        upward = upward + dot_tn(low_up, stack_u[:, piece]).astype(bf16).astype(f32)
        hidden[:, piece] = (gate / (1.0 + jnp.exp(-gate)) * upward).astype(bf16)
    lows = merged(dot_nt(stack_a[...], hidden[...]), masks, rank)
    share(index_ref, hidden[...], down_w, lows, *terms)


def split_pair(rank, kept, *refs):
    *arrived, _, stay, away = refs
    half = len(arrived) // 2
    width = away.shape[1]
    row = 0
    for piece in arrived[:half]:
        here = slice(row, row + piece.shape[0])
        stay[here, :] = kept[here, 0:width] + piece[...].astype(f32)
        row += piece.shape[0]
    row = 0
    for piece in arrived[half:]:
        here = slice(row, row + piece.shape[0])
        away[here, :] = (kept[here, width:] + piece[...].astype(f32)).astype(bf16)
        row += piece.shape[0]
    away[row:, :] = stay[row:, :].astype(bf16)


def finish(first, lens_ref, table, *refs):
    *done, stay, arrived, left, right, out = refs
    row = 0
    for part in done:
        out[row : row + part.shape[0], :] = part[...]
        row += part.shape[0]
    wanted = lens_ref.shape[1]
    half = left.shape[0]
    rows = 2 * half
    masks = lane_masks(lens_ref, wanted, first, rows)
    lows = stay[rows:, 0:rows] + arrived[rows:, 0:rows].astype(f32)
    total = stay[0:rows, :] + arrived[0:rows, :].astype(f32)
    total = total + delta(lows.astype(bf16).astype(f32), masks, table[...])
    for k, piece in enumerate((left, right)):
        at = slice(k * half, (k + 1) * half)
        out[row + k * half : row + (k + 1) * half, :] = (total[at, :] + piece[...].astype(f32)).astype(bf16)


def rotation_tables(lens, row_count):
    half = HEAD_WIDTH // 2
    inverse = rope_base ** (-(jnp.arange(half, dtype=f32) * 2.0) / HEAD_WIDTH)
    row = jnp.arange(row_count, dtype=jnp.int32)
    start_of = jnp.zeros_like(row)
    start = jnp.int32(0)
    for j in range(lens.shape[0]):
        start_of = jnp.where(row >= start, start, start_of)
        start = start + lens[j]
    angle = (row - start_of).astype(f32)[:, None] * jnp.concatenate([inverse, inverse])[None, :]
    sign = jnp.concatenate([-jnp.ones(half, f32), jnp.ones(half, f32)])
    return jnp.cos(angle), jnp.sin(angle) * sign[None, :]


def swap_core(values):
    return lax.ppermute(values, "tp", [(k, k ^ 1) for k in range(4)])


def swap_across(values):
    return lax.ppermute(values, "tp", [(k, k ^ 2) for k in range(4)])


def swap_diagonal(values):
    return lax.ppermute(values, "tp", [(k, k ^ 3) for k in range(4)])


def swap_req(values, flips):
    return lax.ppermute(values, "req", [(k, k ^ flips) for k in range(lax.axis_size("req"))])


def per_device(
    tokens,
    lengths,
    request_adapter_index,
    attention_norm_gain,
    query_norm_gain,
    key_norm_gain,
    feedforward_norm_gain,
    query_weight,
    key_weight,
    value_weight,
    output_weight,
    gate_weight,
    up_weight,
    down_weight,
    query_key_value_adapter_input,
    output_adapter_input,
    gate_up_adapter_input,
    down_adapter_input,
    query_adapter_output,
    key_adapter_output,
    value_adapter_output,
    projection_adapter_output,
    gate_adapter_output,
    up_adapter_output,
    down_adapter_output,
):
    assert lax.axis_size("tp") == 4
    row_count, width = tokens.shape
    groups = lax.axis_size("req")
    wanted = lengths.shape[1]
    held, low_qkv, _ = query_key_value_adapter_input.shape
    rank = output_adapter_input.shape[1]
    low_gu = gate_up_adapter_input.shape[1]
    q_width, k_width = query_weight.shape[1], key_weight.shape[1]
    hidden_width = gate_weight.shape[1]
    heads, kv_heads = q_width // HEAD_WIDTH, k_width // HEAD_WIDTH
    unit = math.gcd(width, hidden_width)
    rows = row_count // CHUNKS
    assert width == q_width == 2 * k_width == row_count
    index = lax.axis_index("tp").astype(jnp.int32).reshape(1)
    me = lax.axis_index("req").astype(jnp.int32).reshape(1)
    want = request_adapter_index

    peers = groups // 2
    across = swap_across(tokens)
    core = swap_core(tokens)
    diagonal = swap_core(across)
    want_neighbour = swap_req(want, 1)

    def for_neighbour(blocks, after, heights):
        return call(
            functools.partial(pick_for_neighbour, len(blocks)),
            [SMEM] * 2 + [VMEM] * len(blocks) + [ANY],
            [shaped((peers, height, blocks[0].shape[2]), bf16) for height in heights],
        )(me, want_neighbour, *blocks, after)

    def loaded(weights, after, limit):
        return call(
            functools.partial(load, len(weights)), [ANY] * (len(weights) + len(after)),
            [shaped(w.shape, bf16) for w in weights],
            scratch=[pltpu.SemaphoreType.DMA((len(weights),))], limit=limit,
        )(*weights, *after)

    tables = (
        query_key_value_adapter_input, query_adapter_output, key_adapter_output, value_adapter_output,
        output_adapter_input, gate_up_adapter_input, projection_adapter_output, down_adapter_output,
        down_adapter_input, gate_adapter_output, up_adapter_output,
    )
    plan = (
        (0, (0, width), 0, 0),
        (1, (0, q_width), low_qkv, 0),
        (2, (0, k_width), low_qkv + rank, 0),
        (3, (0, k_width), low_qkv + rank, k_width),
        (4, (0, width), low_qkv + 2 * rank, 0),
    )
    plan_second, row = [], 0
    shapes = ((low_gu, width), (rank, width), (rank, width)) + ((rank, hidden_width),) * 3
    for table, (height, columns) in enumerate(shapes):
        for k in range(columns // unit):
            plan_second.append((5 + table, (k * unit, unit), row, 0))
            row += height
    block, block_second = call(
        functools.partial(gather_tables, (plan, tuple(plan_second))), [ANY] * len(tables),
        [shaped((held, low_qkv + 3 * rank, width), bf16), shaped((held, row, unit), bf16)],
        scratch=[pltpu.SemaphoreType.DMA((len(plan) + len(plan_second),))], limit=60,
    )(*tables)
    cosine, sine = rotation_tables(lengths[0], row_count)

    gain_one = attention_norm_gain.reshape(1, -1)
    gain_two = feedforward_norm_gain.reshape(1, -1)
    q_gain = query_norm_gain.reshape(1, -1)
    k_gain = key_norm_gain.reshape(1, -1)
    qkv_width = q_width + 2 * k_width
    normed_own, output_weight, *qkv = call(
        project_qkv, [SMEM] + [VMEM] * 5 + [HBM] * 4,
        [shaped((row_count, width), bf16), shaped(output_weight.shape, bf16)] + [shaped((rows, qkv_width), f32)] * CHUNKS,
        scratch=[
            pltpu.VMEM(query_weight.shape, bf16),
            pltpu.VMEM(key_weight.shape, bf16),
            pltpu.VMEM(value_weight.shape, bf16),
            pltpu.SemaphoreType.DMA((13,)),
        ],
        limit=49,
    )(
        index, tokens, core, across, diagonal, gain_one, query_weight, key_weight, value_weight,
        output_weight,
    )
    everyone = [block] + [swap_req(block, 2 * rel) for rel in range(1, peers)]
    everyone[0] = call(hold, [VMEM, ANY], shaped(block.shape, bf16))(block, sine)
    (passing,) = for_neighbour(everyone, sine, [low_qkv + 3 * rank])
    block_second = call(hold, [VMEM, ANY], shaped(block_second.shape, bf16))(block_second, passing)
    second = [block_second] + [swap_req(block_second, 2 * rel) for rel in range(1, peers)]
    low, chosen = call(
        functools.partial(low_first, rank), [SMEM] * 3 + [VMEM] * (peers + 2) + [ANY] * 2,
        [
            shaped((low_qkv, row_count), bf16),
            shaped((wanted, 3 * rank, width), bf16),
        ],
        scratch=[pltpu.VMEM((wanted * low_qkv, width), bf16)],
    )(
        me, want, lengths, *everyone, swap_req(passing, 1), normed_own,
        cosine, sine,
    )
    lows = (low, swap_core(low), swap_across(low), swap_diagonal(low))

    tall = rows + rank
    cuts = [rows // 2, rows // 2 + rank, rows // 2, rows // 2]
    terms = [shaped((tall, 2 * width), f32)] + [shaped((cut, width), bf16) for cut in cuts]
    past = [jnp.zeros((16, k_width), bf16)] * 2
    after = low
    residuals = []
    for c in range(CHUNKS):
        new_k, new_v, keep, *sends = call(
            functools.partial(attend, c, heads, kv_heads),
            [SMEM] * 2 + [VMEM] * 13 + [ANY],
            [shaped((rows, k_width), bf16)] * 2 + terms,
        )(
            index, lengths, qkv[c], *lows, chosen, cosine, sine,
            q_gain, k_gain, output_weight, *past, after,
        )
        past = [new_k, new_v] if c == 0 else [
            jnp.concatenate([old, new], axis=0) for old, new in zip(past, (new_k, new_v))
        ]
        if c == 0:
            heights = [height * (columns // unit) for height, columns in shapes]
            cuts_second = [sum(heights[:2]), sum(heights[2:])]
            passing_second = for_neighbour(second, new_k, cuts_second)
        chip = call(add_pair, [VMEM] * 5 + [ANY] * 3, shaped((tall, 2 * width), bf16))(
            keep, *[swap_core(piece) for piece in sends], passing_second[0] if c == 0 else arrived,
            keep if c == 0 else table_across, keep if c == 0 else gate_weight,
        )
        after = chip
        if c == 0:
            def chosen_second(part, outs, sizes, after):
                return call(
                    functools.partial(choose_second, part * cuts_second[0], peers, sizes),
                    [SMEM] * 2 + [VMEM] * (peers + 1) + [ANY], outs,
                )(me, want, *second, swap_req(passing_second[part], 1), after)

            (table,) = chosen_second(
                0, [shaped((wanted * (low_gu + rank), width), bf16)],
                ((0, 0, low_gu), (0, wanted * low_gu, rank)), chip,
            )
            gate_weight, up_weight, down_weight = loaded(
                (gate_weight, up_weight, down_weight), (table,), 44
            )
            down_b, down_a, gate_b, up_b = chosen_second(
                1, [shaped((wanted * h, w), bf16) for h, w in shapes[2:]],
                tuple((k, 0, h) for k, (h, _) in enumerate(shapes[2:])), table,
            )
            table_across = swap_across(table)
            tables = (table, swap_core(table), table_across, swap_core(table_across))
        arrived = swap_across(chip)
        resid = call(
            functools.partial(residual, c), [SMEM] + [VMEM] * 6 + [ANY],
            [shaped((rows // 2, width), bf16)] * 4,
        )(
            lengths, chip, arrived, tokens, across, table, table_across, gate_weight,
        )
        residuals.append(resid)

    done = []
    arrived = gate_weight
    for c in range(CHUNKS):
        resid = residuals[c]
        keep, *sends = call(
            functools.partial(feed_forward, c),
            [SMEM] * 2 + [VMEM] * 19,
            terms,
            limit=32,
            scratch=[
                pltpu.VMEM((rows, 4 * width), bf16),
                pltpu.VMEM((rows, hidden_width), bf16),
            ],
        )(
            index, lengths, *resid, *[swap_core(piece) for piece in resid], *tables, down_a, gate_b, up_b,
            gain_two, gate_weight, up_weight, down_weight,
        )
        stay, away = call(
            functools.partial(split_pair, rank), [VMEM] * 5 + [ANY],
            [shaped((tall, width), f32), shaped((tall, width), bf16)],
        )(keep, *[swap_core(piece) for piece in sends], arrived)
        after = away
        arrived = swap_across(away)
        last = c == CHUNKS - 1
        before = done if last else []
        done.append(
            call(
                functools.partial(finish, c * rows), [SMEM] + [VMEM] * (5 + len(before)),
                shaped((row_count if last else rows, width), bf16),
            )(lengths, down_b, *before, stay, arrived, *resid[:2])
        )
    return done[-1]


def solution(mesh):
    placed = (
        P("req", "tp"),
        P("req", None),
        P("req", None),
        P(),
        P(),
        P(),
        P(),
        P(None, "tp"),
        P(None, "tp"),
        P(None, "tp"),
        P("tp", None),
        P(None, "tp"),
        P(None, "tp"),
        P("tp", None),
        P("req", None, "tp"),
        P("req", None, "tp"),
        P("req", None, "tp"),
        P("req", None, "tp"),
        P("req", None, "tp"),
        P("req", None, "tp"),
        P("req", None, "tp"),
        P("req", None, "tp"),
        P("req", None, "tp"),
        P("req", None, "tp"),
        P("req", None, "tp"),
    )
    return jax.shard_map(
        per_device, mesh=mesh, in_specs=placed, out_specs=P("req", "tp"), check_vma=False
    )
```
